512 devices in a mesh: dp: 8 (over y_lo, x), shard: 64 (over z, y_hi, core).
Axes of the slice: x: 4, y: 4 (y_hi: 2, y_lo: 2; y = y_hi * 2 + y_lo), z: 16, core: 2. Of those that a mesh axis runs over, the one named last changes fastest.
Arguments:
- edge_feats: bfloat16 [65536, 1024], P(('dp', 'shard')), may hold values from -6 to 6
- edge_dst: int32 [65536], P(('dp', 'shard')), may hold values from 0 to 127
- edge_live: int32 [512], P(('dp', 'shard')), may hold values from 64 to 128, as said below
- coefficients: float32 [128, 32], P('dp'), may hold values from 0.01 to 0.5
- expert_weights: float32 [32, 524288], P(None, 'shard'), may hold values from -0.1875 to 0.1875
- node_cot: bfloat16 [65536, 1024], P(('dp', 'shard')), may hold values from -6 to 6
Outputs:
- node_out: bfloat16 [65536, 1024], P(('dp', 'shard'))
- edge_grad: bfloat16 [65536, 1024], P(('dp', 'shard'))
- weight_grad: float32 [32, 524288], P(None, 'shard')
- coef_grad: float32 [128, 32], P('dp')
The draws below stay inside these ranges and needn't reach their ends.
Inputs may be any that keep to these rules, and one draw needn't show every extreme that they name: On each device the first edge_live slots of its 128 edge slots are live and the rest are padding; some device has all 128 slots live in every draw.
All inputs are finite; a program needn't handle non-finite values.
Results may differ from the reference program's by a relative error of at most 0.0062.
Values may be sent and summed in bfloat16 or wider, within the bound.
A program may use at most 64 MiB of HBM per device.

```python
import math
import jax
import jax.numpy as jnp
from jax import lax

EXPERTS = 32
DEV_CRYS = 4
EDGE_DEV = 128
ATOM_DEV = 128
K = 512
PARAMS = 524288
CRYSTALS = 128
EDGES = 65536
ATOMS = 65536
DEVICES = 512


def draw_edge_live(key, part):
    key = jax.random.fold_in(key, 3)
    first_key, second_key = jax.random.split(key)
    counts = jax.random.randint(first_key, (DEVICES,), EDGE_DEV // 2, EDGE_DEV + 1)
    fullest = jax.random.randint(second_key, (), 0, DEVICES)
    return jnp.where(jnp.arange(DEVICES) == fullest, EDGE_DEV, counts).astype(jnp.int32)


def touch_ends(array, stream_key, smallest, high):
    spot = [jax.random.randint(jax.random.fold_in(stream_key, axis), (), 0, length) for axis, length in enumerate(array.shape)]
    longest = array.shape.index(max(array.shape))
    next_to = spot[:longest] + [(spot[longest] + 1) % array.shape[longest]] + spot[longest + 1:]
    return array.at[tuple(spot)].set(smallest).at[tuple(next_to)].set(high)


def level_of(key, dims, cuts, smallest, largest):
    def one(position, parts):
        steps = jax.random.uniform(jax.random.fold_in(jax.random.fold_in(key, 6), position), (parts,), jnp.float32, smallest / len(cuts), largest / len(cuts))
        return jnp.repeat(jnp.exp(steps), dims[position] // parts).reshape((-1,) + (1,) * (len(dims) - position - 1))

    factor_of = one(*cuts[0])
    for cut in cuts[1:]:
        factor_of = factor_of * one(*cut)
    return factor_of


def bell_draw(rng, dims, width, bound, cuts=(), kind=jnp.bfloat16):
    values = jax.random.normal(rng, dims, jnp.float32) * width
    if len(cuts) > 0:
        values = level_of(rng, dims, cuts, -0.22, 0.18) * values
    return jnp.clip(values, min=-bound, max=bound).astype(kind)


def setup_inputs(seed: int = 0) -> dict:
    key_of = jax.random.split(jax.random.key(seed), 7)
    edge_feats = bell_draw(key_of[0], (EDGES, 2 * K), 1.0, 6.0, ((0, 512),))
    edge_dst = touch_ends(jax.random.randint(key_of[1], (EDGES,), 0, ATOM_DEV), jax.random.fold_in(key_of[1], 1), 0, ATOM_DEV - 1).astype(jnp.int32)
    edge_live = draw_edge_live(jax.random.fold_in(key_of[6], 71), 0)
    coefficients = jnp.clip(jnp.exp(math.log(0.5) - 3.912023 * jax.random.uniform(key_of[3], (CRYSTALS, EXPERTS), jnp.float32) ** level_of(key_of[3], (CRYSTALS, EXPERTS), ((0, 8),), -0.2, 0.2)), 0.01, 0.5)
    expert_weights = bell_draw(key_of[4], (EXPERTS, PARAMS), (2 * K) ** -0.5, 0.1875, ((1, 64),), jnp.float32)
    node_cot = bell_draw(key_of[5], (ATOMS, 2 * K), 1.0, 6.0, ((0, 512),))
    return dict(edge_feats=edge_feats, edge_dst=edge_dst, edge_live=edge_live, coefficients=coefficients, expert_weights=expert_weights, node_cot=node_cot)


def complex_block(flattened):
    square = K * K
    real_part = flattened[:square].reshape(K, K)
    imag_part = flattened[square:].reshape(K, K)
    upper_half = jnp.concatenate([real_part, imag_part], axis=1)
    lower_half = jnp.concatenate([-imag_part, real_part], axis=1)
    return jnp.concatenate([upper_half, lower_half], axis=0)


def reference(edge_feats, edge_dst, edge_live, coefficients, expert_weights, node_cot):
    feature_width = 2 * K
    copies = lax.optimization_barrier(expert_weights.astype(jnp.bfloat16)).astype(jnp.float32)
    feats = edge_feats.reshape(CRYSTALS, DEV_CRYS * EDGE_DEV, feature_width)
    targets = edge_dst.reshape(CRYSTALS, DEV_CRYS, EDGE_DEV)
    counts = edge_live.reshape(CRYSTALS, DEV_CRYS)
    cotangent = node_cot.reshape(CRYSTALS, DEV_CRYS, ATOM_DEV, feature_width)
    slot_index = jnp.arange(EDGE_DEV, dtype=jnp.int32)
    atom_index = jnp.arange(ATOM_DEV, dtype=jnp.int32)

    def one_crystal(running, sliced):
        coef_row, flattened_feats, target_row, count_row, cot_row = sliced
        merged = jnp.dot(coef_row[None, :], copies, precision=lax.Precision.HIGHEST)[0].astype(jnp.bfloat16)
        block_matrix = complex_block(merged)
        kept_slots = slot_index[None, :] < count_row[:, None]
        selector = ((target_row[:, None, :] == atom_index[None, :, None]) & kept_slots[:, None, :]).astype(jnp.float32)
        messages = jnp.dot(flattened_feats, block_matrix, preferred_element_type=jnp.float32)
        messages = messages.reshape(DEV_CRYS, EDGE_DEV, feature_width)
        messages = jnp.where(kept_slots[:, :, None], messages, 0.0).astype(jnp.bfloat16)
        node_sum = jnp.einsum("dae,dew->daw", selector, messages.astype(jnp.float32)).astype(jnp.bfloat16)
        edge_cot = jnp.einsum("dae,daw->dew", selector, cot_row.astype(jnp.float32)).astype(jnp.bfloat16)
        edge_cot = edge_cot.reshape(DEV_CRYS * EDGE_DEV, feature_width)
        grad_rows = jnp.dot(edge_cot, block_matrix.T, preferred_element_type=jnp.float32).astype(jnp.bfloat16)
        outer = jnp.dot(flattened_feats.T, edge_cot, preferred_element_type=jnp.float32)
        real_grad = outer[:K, :K] + outer[K:, K:]
        imag_grad = outer[:K, K:] - outer[K:, :K]
        merged_grad = jnp.concatenate([real_grad.reshape(-1), imag_grad.reshape(-1)]) / EDGE_DEV
        running = running + coef_row[:, None] * merged_grad[None, :]
        coef_part = jnp.dot(copies, merged_grad, precision=lax.Precision.HIGHEST)
        return running, (node_sum, grad_rows, coef_part)

    start = jnp.zeros((EXPERTS, PARAMS), jnp.float32)
    weight_grad, stacked = lax.scan(one_crystal, start, (coefficients, feats, targets, counts, cotangent))
    node_out = stacked[0].reshape(ATOMS, feature_width)
    edge_grad = stacked[1].reshape(EDGES, feature_width)
    coef_grad = stacked[2]
    return node_out, edge_grad, weight_grad, coef_grad
```

```python
import jax
import jax.numpy as jnp
from jax import lax
from jax.experimental import pallas as pl
from jax.experimental.pallas import tpu as pltpu
from jax.sharding import PartitionSpec as P

F32, BF16 = jnp.float32, jnp.bfloat16
NZ, NQ, NG = 16, 4, 8
NX = 4
ROWS, COLS = 16, 512
EDGES, WIDTH, EXPERTS = 128, 1024, 32
YC = 4
DMA = pltpu.SemaphoreType.DMA


def three_parts(value):
    high = value.astype(BF16)
    rest = value - high.astype(F32)
    middle = rest.astype(BF16)
    low = (rest - middle.astype(F32)).astype(BF16)
    return high, middle, low


def tn_dot(a, b):
    return lax.dot_general(a, b, (((0,), (0,)), ((), ())), preferred_element_type=F32)


def nt_dot(a, b):
    return lax.dot_general(a, b, (((1,), (1,)), ((), ())), preferred_element_type=F32)


def kernel(
    feats_in, dst_in, live_in, coef_in, weights_in, cot_in,
    node_out, edge_grad, weight_out, coef_out,
    weights, copies, merged_rows, merged_send, block, feats, node_cot, edge_cot,
    grads, y_send, y_recv, dp_send, dp_recv, z_send, z_recv, crystals, gather,
    gather_send, coef_all, coef_rows, part, part_send, part_recv, sum_send, sum_recv, last,
    in_sem, fz_s, fz_r, fy_s, fy_r, fc_s, fc_r, gc_s, gc_r, ex_s, ex_r, co_s, co_r,
    ys_s, ys_r, da_s, da_r, bz_s, bz_r, ag_s, ag_r, cd_s, cd_r, cz_s, cz_r, cl_s, cl_r,
):
    g = lax.axis_index("dp")
    s = lax.axis_index("shard")
    z = s // NQ
    q = s % NQ
    yh = q // 2
    core = q % 2
    h = g // NX
    x = g % NX
    core_peer = z * NQ + yh * 2 + (1 - core)
    y_peer = z * NQ + (1 - yh) * 2 + core

    def shard_copy(src, dst, send, recv, peer):
        return pltpu.make_async_remote_copy(
            src_ref=src, dst_ref=dst, send_sem=send, recv_sem=recv,
            device_id={"dp": g, "shard": peer}, device_id_type=pl.DeviceIdType.MESH,
        )

    def dp_copy(src, dst, send, recv, peer):
        return pltpu.make_async_remote_copy(
            src_ref=src, dst_ref=dst, send_sem=send, recv_sem=recv,
            device_id={"dp": peer, "shard": s}, device_id_type=pl.DeviceIdType.MESH,
        )

    load_w = pltpu.make_async_copy(weights_in, weights, in_sem.at[0])
    load_f = pltpu.make_async_copy(feats_in, feats.at[0], in_sem.at[1])
    load_c = pltpu.make_async_copy(cot_in, node_cot, in_sem.at[2])
    load_w.start()
    load_f.start()
    load_c.start()

    barrier = pltpu.get_barrier_semaphore()

    def greet_shard(peer):
        pl.semaphore_signal(
            barrier, inc=1, device_id={"dp": g, "shard": peer}, device_id_type=pl.DeviceIdType.MESH
        )

    greet_shard(core_peer)
    greet_shard(y_peer)

    @pl.loop(1, NZ)
    def _(off):
        greet_shard(((z + off) % NZ) * NQ + q)

    @pl.loop(1, NG)
    def _(off):
        pl.semaphore_signal(
            barrier, inc=1, device_id={"dp": (g + off) % NG, "shard": s}, device_id_type=pl.DeviceIdType.MESH
        )

    coef = coef_in[...]
    stacked = jnp.concatenate(three_parts(coef), axis=0)
    coef_all[g] = jnp.concatenate([coef, jnp.zeros((NZ, 128 - EXPERTS), F32)], axis=1)
    load_w.wait()
    for row in range(ROWS):
        lanes = pl.ds(row * COLS, COLS)
        rounded = weights[:, lanes].astype(BF16)
        copies[:, lanes] = rounded
        terms = jnp.dot(stacked, rounded, preferred_element_type=F32)
        merged_rows[:, row, :] = terms[0:NZ] + terms[NZ : 2 * NZ] + terms[2 * NZ : 3 * NZ]
    merged_send[...] = merged_rows[...].astype(BF16)

    pl.semaphore_wait(barrier, 2 + (NZ - 1) + (NG - 1))

    def fz(off):
        to = (z + off) % NZ
        return shard_copy(merged_send.at[to], block.at[z, q], fz_s.at[off], fz_r.at[off], to * NQ + q)

    def fz_in(off):
        at = (z + NZ - off) % NZ
        return shard_copy(merged_send.at[at], block.at[at, q], fz_s.at[off], fz_r.at[off], at * NQ + q)

    @pl.loop(1, NZ)
    def _(off):
        fz(off).start()

    block[z, q] = merged_send[z]

    load_f.wait()
    feats_copy = shard_copy(feats.at[0], feats.at[1], ex_s.at[0], ex_r.at[0], core_peer)
    feats_copy.start()
    atom = lax.broadcasted_iota(jnp.int32, (EDGES, EDGES), 0)
    slot = lax.broadcasted_iota(jnp.int32, (EDGES, EDGES), 1)
    chosen = (dst_in[...] == atom) & (slot < live_in[0])
    selector = jnp.where(chosen, 1.0, 0.0).astype(BF16)
    load_c.wait()
    edge_cot[0] = tn_dot(selector, node_cot[...]).astype(BF16)
    cot_copy = shard_copy(edge_cot.at[0], edge_cot.at[1], ex_s.at[1], ex_r.at[1], core_peer)
    cot_copy.start()

    def co(off):
        to = (g + off) % NG
        return dp_copy(coef_all.at[g], coef_all.at[g], co_s.at[off], co_r.at[off], to)

    def co_in(off):
        at = (g + NG - off) % NG
        return dp_copy(coef_all.at[at], coef_all.at[at], co_s.at[off], co_r.at[off], at)

    @pl.loop(1, NG)
    def _(off):
        co(off).start()

    feats_copy.wait_recv()
    cot_copy.wait_recv()
    half = WIDTH // 2
    left, right = [], []
    for device in range(2):
        f, c = feats[device], edge_cot[device]
        left += [f[:, :half], f[:, half:]]
        right += [
            jnp.concatenate([c[:, :half], c[:, half:]], axis=1),
            jnp.concatenate([c[:, half:], -c[:, :half]], axis=1),
        ]
    outer = tn_dot(jnp.concatenate(left, axis=0), jnp.concatenate(right, axis=0)) * (1.0 / EDGES)
    grads[0 : NZ // 2] = outer[:, :half].reshape(NZ // 2, 2, 2, ROWS, COLS)
    grads[NZ // 2 : NZ] = outer[:, half:].reshape(NZ // 2, 2, 2, ROWS, COLS)
    y_send[...] = grads[:, 1 - yh, core].astype(BF16)

    per = NZ // YC

    def ys(chunk):
        at = pl.ds(chunk * per, per)
        return shard_copy(y_send.at[at], y_recv.at[at], ys_s.at[chunk], ys_r.at[chunk], y_peer)

    for chunk in range(YC):
        ys(chunk).start()

    def fy(off):
        at = (z + NZ - off) % NZ
        return shard_copy(block.at[at, q], block.at[at, q], fy_s.at[off], fy_r.at[off], y_peer)

    def fc(off):
        at = (z + NZ - off) % NZ
        return shard_copy(block.at[at, q], block.at[at, q], fc_s.at[off], fc_r.at[off], core_peer)

    q_y = (1 - yh) * 2 + core
    q_c = yh * 2 + (1 - core)
    q_yc = (1 - yh) * 2 + (1 - core)

    def fy_in(off):
        at = (z + NZ - off) % NZ
        return shard_copy(block.at[at, q_y], block.at[at, q_y], fy_s.at[off], fy_r.at[off], y_peer)

    def fc_in(off):
        at = (z + NZ - off) % NZ
        return shard_copy(block.at[at, q_c], block.at[at, q_c], fc_s.at[off], fc_r.at[off], core_peer)

    def gc(off):
        at = (z + NZ - off) % NZ
        return shard_copy(block.at[at, q_y], block.at[at, q_y], gc_s.at[off], gc_r.at[off], core_peer)

    def gc_in(off):
        at = (z + NZ - off) % NZ
        return shard_copy(block.at[at, q_yc], block.at[at, q_yc], gc_s.at[off], gc_r.at[off], core_peer)

    fy(0).start()
    fc(0).start()

    def forward(low, high):
        @pl.loop(low, high)
        def _(step):
            for off in (step, NZ - step):
                fz_in(off).wait_recv()
                fy(off).start()
                fc(off).start()

    forward(1, 4)

    for chunk in range(YC):
        ys(chunk).wait_recv()
    for p in range(NZ // 2):
        low = grads[p, yh, core] + y_recv[p].astype(F32)
        high = grads[p + NZ // 2, yh, core] + y_recv[p + NZ // 2].astype(F32)
        for to in range(NG):
            rows = slice((to // NX) * 8, (to // NX) * 8 + 8)
            lanes = slice((to % NX) * 128, (to % NX) * 128 + 128)
            dp_send[to, p] = jnp.concatenate([low[rows, lanes], high[rows, lanes]], axis=0).astype(BF16)

    def da(off):
        to = (g + off) % NG
        return dp_copy(dp_send.at[to], dp_recv.at[g], da_s.at[off], da_r.at[off], to)

    def da_in(off):
        at = (g + NG - off) % NG
        return dp_copy(dp_send.at[at], dp_recv.at[at], da_s.at[off], da_r.at[off], at)

    @pl.loop(1, NG)
    def _(off):
        da(off).start()

    dp_recv[g] = dp_send[g]

    forward(4, 8)
    fz_in(8).wait_recv()
    fy(8).start()
    fc(8).start()

    @pl.loop(1, NG)
    def _(off):
        da_in(off).wait_recv()

    for p in range(NZ // 2):
        for j in range(NG // 2):
            even = dp_recv[2 * j, p].astype(F32)
            odd = dp_recv[2 * j + 1, p].astype(F32)
            z_send[p, j] = jnp.concatenate([even[:8], odd[:8]], axis=0).astype(BF16)
            z_send[p + NZ // 2, j] = jnp.concatenate([even[8:], odd[8:]], axis=0).astype(BF16)

    def bz(off):
        to = (z + off) % NZ
        return shard_copy(z_send.at[to], z_recv.at[z], bz_s.at[off], bz_r.at[off], to * NQ + q)

    def bz_in(off):
        at = (z + NZ - off) % NZ
        return shard_copy(z_send.at[at], z_recv.at[at], bz_s.at[off], bz_r.at[off], at * NQ + q)

    @pl.loop(1, NZ)
    def _(off):
        bz(off).start()

    z_recv[z] = z_send[z]

    @pl.loop(0, NZ)
    def _(off):
        fy_in(off).wait_recv()
        gc(off).start()

    @pl.loop(0, NZ)
    def _(off):
        fc_in(off).wait_recv()
        gc_in(off).wait_recv()

    matrix = block[...].reshape(NZ * NQ * ROWS, COLS)
    f = feats[0]
    lifted = jnp.concatenate(
        [
            jnp.concatenate([f[:, :half], -f[:, half:]], axis=1),
            jnp.concatenate([f[:, half:], f[:, :half]], axis=1),
        ],
        axis=0,
    )
    messages = jnp.dot(lifted, matrix, preferred_element_type=F32).astype(BF16)
    messages = jnp.concatenate([messages[:EDGES], messages[EDGES:]], axis=1)
    node_out[...] = jnp.dot(selector, messages, preferred_element_type=F32).astype(BF16)
    c = edge_cot[0]
    products = nt_dot(jnp.concatenate([c[:, :half], c[:, half:]], axis=0), matrix)
    edge_grad[:, :half] = (products[:EDGES, :half] + products[EDGES:, half:]).astype(BF16)
    edge_grad[:, half:] = (products[EDGES:, :half] - products[:EDGES, half:]).astype(BF16)

    @pl.loop(1, NG)
    def _(off):
        co_in(off).wait_recv()

    for group in range(NG):
        coef_rows[:, group, :] = coef_all[group]
    all_coef = coef_rows[...].reshape(NZ * NG, 128)[:, :EXPERTS]
    all_parts = jnp.concatenate(three_parts(all_coef), axis=1)

    @pl.loop(1, NZ)
    def _(off):
        bz_in(off).wait_recv()

    crystals[...] = z_recv[...].astype(F32).reshape(NZ * NG, 8, 128)
    flat = jnp.concatenate([crystals[:, row, :] for row in range(8)], axis=1).astype(BF16)
    terms = tn_dot(all_parts, flat)
    total = (terms[:EXPERTS] + terms[EXPERTS : 2 * EXPERTS] + terms[2 * EXPERTS :]).astype(BF16)
    for row in range(8):
        gather_send[row] = total[:, row * 128 : row * 128 + 128]

    def ag(off):
        to = (g + off) % NG
        return dp_copy(gather_send, gather.at[pl.ds(h * 8, 8), x], ag_s.at[off], ag_r.at[off], to)

    def ag_in(off):
        at = (g + NG - off) % NG
        return dp_copy(gather_send, gather.at[pl.ds((at // NX) * 8, 8), at % NX], ag_s.at[off], ag_r.at[off], at)

    @pl.loop(1, NG)
    def _(off):
        ag(off).start()

    gather[pl.ds(h * 8, 8), x] = gather_send[...]

    own = jnp.concatenate(
        [
            copies[:, pl.ds(pl.multiple_of((h * 8 + row) * COLS + x * 128, 128), 128)]
            for row in range(8)
        ],
        axis=1,
    )
    total_part = jnp.zeros((4 * NG, 128), F32)
    zero = jnp.zeros_like(own)
    for b in range(4):
        rows = jnp.concatenate(
            [flat[(4 * a + b) * NG : (4 * a + b) * NG + NG] for a in range(4)], axis=0
        )
        placed = jnp.concatenate([own if k == b else zero for k in range(4)], axis=0)
        total_part = total_part + nt_dot(rows, placed)
    part[...] = total_part.reshape(4, NG, 128)
    empty = jnp.zeros((4, 128), F32)
    for group in range(NG):
        part_send[group] = jnp.concatenate([part[:, group, :], empty], axis=0)

    def cd(off):
        to = (g + off) % NG
        return dp_copy(part_send.at[to], part_recv.at[g], cd_s.at[off], cd_r.at[off], to)

    def cd_in(off):
        at = (g + NG - off) % NG
        return dp_copy(part_send.at[at], part_recv.at[at], cd_s.at[off], cd_r.at[off], at)

    @pl.loop(1, NG)
    def _(off):
        cd(off).start()

    part_recv[g] = part_send[g]

    @pl.loop(1, NG)
    def _(off):
        cd_in(off).wait_recv()

    sum_send[...] = jnp.sum(part_recv[...], axis=0)

    def cz(off):
        to = (z + off) % NZ
        return shard_copy(sum_send, sum_recv.at[z], cz_s.at[off], cz_r.at[off], to * NQ + q)

    def cz_in(off):
        at = (z + NZ - off) % NZ
        return shard_copy(sum_send, sum_recv.at[at], cz_s.at[off], cz_r.at[off], at * NQ + q)

    @pl.loop(1, NZ)
    def _(off):
        cz(off).start()

    sum_recv[z] = sum_send[...]

    @pl.loop(1, NZ)
    def _(off):
        cz_in(off).wait_recv()

    last[0] = jnp.sum(sum_recv[...], axis=0)
    core_copy = shard_copy(last.at[0], last.at[1], cl_s.at[0], cl_r.at[0], core_peer)
    core_copy.start()
    core_copy.wait_recv()
    last[2] = last[0] + last[1]
    y_copy = shard_copy(last.at[2], last.at[3], cl_s.at[1], cl_r.at[1], y_peer)
    y_copy.start()
    y_copy.wait_recv()
    summed = (last[2] + last[3])[:4]
    coef_out[...] = jnp.concatenate(
        [summed[a : a + 1, b * EXPERTS : (b + 1) * EXPERTS] for a in range(4) for b in range(4)], axis=0
    )

    @pl.loop(1, NG)
    def _(off):
        ag_in(off).wait_recv()

    for row in range(ROWS):
        for tile in range(NX):
            weight_out[:, pl.ds((row * NX + tile) * 128, 128)] = gather[row, tile]

    @pl.loop(1, NZ)
    def _(off):
        fz(off).wait_send()
        bz(off).wait_send()
        cz(off).wait_send()

    @pl.loop(0, NZ)
    def _(off):
        fy(off).wait_send()
        fc(off).wait_send()
        gc(off).wait_send()

    @pl.loop(1, NG)
    def _(off):
        co(off).wait_send()
        da(off).wait_send()
        ag(off).wait_send()
        cd(off).wait_send()

    feats_copy.wait_send()
    cot_copy.wait_send()
    core_copy.wait_send()
    y_copy.wait_send()
    for chunk in range(YC):
        ys(chunk).wait_send()


def per_device(edge_feats, edge_dst, edge_live, coefficients, expert_weights, node_cot):
    vmem = pl.BlockSpec(memory_space=pltpu.VMEM)
    smem = pl.BlockSpec(memory_space=pltpu.SMEM)
    hbm = pl.BlockSpec(memory_space=pl.ANY)
    node_out, edge_grad, weight_grad, coef_grad = pl.pallas_call(
        kernel,
        out_shape=(
            jax.ShapeDtypeStruct((EDGES, WIDTH), BF16),
            jax.ShapeDtypeStruct((EDGES, WIDTH), BF16),
            jax.ShapeDtypeStruct((EXPERTS, ROWS * COLS), BF16),
            jax.ShapeDtypeStruct((NZ, EXPERTS), F32),
        ),
        in_specs=[hbm, vmem, smem, vmem, hbm, hbm],
        out_specs=(vmem, vmem, vmem, vmem),
        scratch_shapes=[
            pltpu.VMEM((EXPERTS, ROWS * COLS), F32),
            pltpu.VMEM((EXPERTS, ROWS * COLS), BF16),
            pltpu.VMEM((NZ, ROWS, COLS), F32),
            pltpu.VMEM((NZ, ROWS, COLS), BF16),
            pltpu.VMEM((NZ, NQ, ROWS, COLS), BF16),
            pltpu.VMEM((2, EDGES, WIDTH), BF16),
            pltpu.VMEM((EDGES, WIDTH), BF16),
            pltpu.VMEM((2, EDGES, WIDTH), BF16),
            pltpu.VMEM((NZ, 2, 2, ROWS, COLS), F32),
            pltpu.VMEM((NZ, ROWS, COLS), BF16),
            pltpu.VMEM((NZ, ROWS, COLS), BF16),
            pltpu.VMEM((NG, NZ // 2, 16, 128), BF16),
            pltpu.VMEM((NG, NZ // 2, 16, 128), BF16),
            pltpu.VMEM((NZ, NG // 2, 16, 128), BF16),
            pltpu.VMEM((NZ, NG // 2, 16, 128), BF16),
            pltpu.VMEM((NZ * NG, 8, 128), F32),
            pltpu.VMEM((ROWS, NX, EXPERTS, 128), BF16),
            pltpu.VMEM((8, EXPERTS, 128), BF16),
            pltpu.VMEM((NG, NZ, 128), F32),
            pltpu.VMEM((NZ, NG, 128), F32),
            pltpu.VMEM((4, NG, 128), F32),
            pltpu.VMEM((NG, 8, 128), F32),
            pltpu.VMEM((NG, 8, 128), F32),
            pltpu.VMEM((8, 128), F32),
            pltpu.VMEM((NZ, 8, 128), F32),
            pltpu.VMEM((4, 8, 128), F32),
            DMA((3,)),
            DMA((NZ,)), DMA((NZ,)), DMA((NZ,)), DMA((NZ,)), DMA((NZ,)), DMA((NZ,)), DMA((NZ,)), DMA((NZ,)),
            DMA((2,)), DMA((2,)), DMA((NG,)), DMA((NG,)),
            DMA((YC,)), DMA((YC,)), DMA((NG,)), DMA((NG,)), DMA((NZ,)), DMA((NZ,)),
            DMA((NG,)), DMA((NG,)), DMA((NG,)), DMA((NG,)), DMA((NZ,)), DMA((NZ,)), DMA((2,)), DMA((2,)),
        ],
        compiler_params=pltpu.CompilerParams(
            collective_id=0, has_side_effects=True, vmem_limit_bytes=40 * 1024 * 1024
        ),
    )(edge_feats, edge_dst.reshape(1, EDGES), edge_live, coefficients, expert_weights, node_cot)
    return node_out, edge_grad, weight_grad.astype(F32), coef_grad


def solution(mesh):
    in_specs = (
        P(("dp", "shard"), None),
        P(("dp", "shard")),
        P(("dp", "shard")),
        P("dp", None),
        P(None, "shard"),
        P(("dp", "shard"), None),
    )
    out_specs = (
        P(("dp", "shard"), None),
        P(("dp", "shard"), None),
        P(None, "shard"),
        P("dp", None),
    )
    return jax.shard_map(
        per_device, mesh=mesh, in_specs=in_specs, out_specs=out_specs, check_vma=False
    )
```

```python
import jax
import jax.numpy as jnp
from jax import lax
from jax.experimental import pallas as pl
from jax.experimental.pallas import tpu as pltpu
from jax.sharding import PartitionSpec as P

F32, BF16 = jnp.float32, jnp.bfloat16
NZ, NQ, NG = 16, 4, 8
NX = 4
ROWS, COLS = 16, 512
EDGES, WIDTH, EXPERTS = 128, 1024, 32
YC = 4
PER = NZ // YC
OFFS = [8, 7, 9, 6, 10, 5, 11, 4, 12, 3, 13, 2, 14, 1, 15, 0]
FAR = 5
GROUPS = [[0, 8, 7, 9, 6, 10], [5, 11, 4, 12], [3, 13], [2, 14], [1, 15]]
GROUP_OF = {off: group for group, offs in enumerate(GROUPS) for off in offs}
DMA = pltpu.SemaphoreType.DMA


def three_parts(value):
    high = value.astype(BF16)
    rest = value - high.astype(F32)
    middle = rest.astype(BF16)
    low = (rest - middle.astype(F32)).astype(BF16)
    return high, middle, low


def tn_dot(a, b):
    return lax.dot_general(a, b, (((0,), (0,)), ((), ())), preferred_element_type=F32)


def nt_dot(a, b):
    return lax.dot_general(a, b, (((1,), (1,)), ((), ())), preferred_element_type=F32)


def kernel(
    feats_in, dst_in, live_in, coef_in, weights_in, cot_in,
    node_out, edge_grad, weight_out, coef_out,
    weights, copies, coef, dst, merged_rows, merged_send, block, feats, node_cot, edge_cot,
    grads, y_send, y_recv, z_send, z_recv, z_wide, dp_send, dp_recv, crystals, gather,
    gather_send, coef_all, planes, part, sum_send, sum_recv,
    node_rows, grad_rows, weight_rows,
    in_sem, out_sem, fz_s, fz_r, fy_s, fy_r, fc_s, fc_r, gc_s, gc_r, ex_s, ex_r, co_s, co_r,
    ys_s, ys_r, bz_s, bz_r, da_s, da_r, ag_s, ag_r, cz_s, cz_r, pt_s, pt_r,
):
    g = lax.axis_index("dp")
    s = lax.axis_index("shard")
    z = s // NQ
    q = s % NQ
    yh = q // 2
    core = q % 2
    h = g // NX
    x = g % NX
    q_y = (1 - yh) * 2 + core
    q_c = yh * 2 + (1 - core)
    q_yc = (1 - yh) * 2 + (1 - core)
    core_peer = z * NQ + q_c
    y_peer = z * NQ + q_y
    half = WIDTH // 2

    load_w = pltpu.make_async_copy(weights_in, weights, in_sem.at[0])
    load_f = pltpu.make_async_copy(feats_in, feats.at[0], in_sem.at[1])
    load_c = pltpu.make_async_copy(cot_in, node_cot, in_sem.at[2])
    load_k = pltpu.make_async_copy(coef_in, coef, in_sem.at[3])
    load_d = pltpu.make_async_copy(dst_in, dst, in_sem.at[4])
    for load in (load_w, load_k, load_d, load_c, load_f):
        load.start()

    def copy_to(src, dst, send, recv, dp, shard):
        return pltpu.make_async_remote_copy(
            src_ref=src, dst_ref=dst, send_sem=send, recv_sem=recv,
            device_id={"dp": dp, "shard": shard}, device_id_type=pl.DeviceIdType.MESH,
        )

    def shard_copy(src, dst, send, recv, peer):
        return copy_to(src, dst, send, recv, g, peer)

    def dp_copy(src, dst, send, recv, peer):
        return copy_to(src, dst, send, recv, peer, s)

    def sent(ref, sem):
        shard_copy(ref, ref, sem, sem, core_peer).wait_send()

    def arrived(ref, sem):
        shard_copy(ref, ref, sem, sem, core_peer).wait_recv()

    def ahead(off):
        return (z + off) % NZ

    def behind(off):
        return (z + NZ - off) % NZ

    barrier = pltpu.get_barrier_semaphore()

    def greet(dp, shard):
        pl.semaphore_signal(
            barrier, inc=1, device_id={"dp": dp, "shard": shard}, device_id_type=pl.DeviceIdType.MESH
        )

    for off in OFFS[:-1]:
        greet(g, ahead(off) * NQ + q)
    for off in range(1, NG):
        greet((g + off) % NG, s)
    greet(g, core_peer)
    greet(g, y_peer)

    load_k.wait()
    stacked = jnp.concatenate(three_parts(coef[...]), axis=0)
    blank = jnp.zeros((1, 128 - EXPERTS), F32)
    for j in range(NZ):
        row = coef[pl.ds(behind(OFFS[j]), 1), :]
        coef_all[g, pl.ds(j, 1), :] = jnp.concatenate([row, blank], axis=1)
    load_w.wait()
    for row in range(ROWS):
        lanes = pl.ds(row * COLS, COLS)
        rounded = weights[:, lanes].astype(BF16)
        copies[:, lanes] = rounded
        terms = jnp.dot(stacked, rounded, preferred_element_type=F32)
        merged_rows[:, row, :] = terms[0:NZ] + terms[NZ : 2 * NZ] + terms[2 * NZ : 3 * NZ]
    merged_send[...] = merged_rows[...].astype(BF16)
    block[z, q] = merged_send[z]

    load_d.wait()
    atom = lax.broadcasted_iota(jnp.int32, (EDGES, EDGES), 0)
    slot = lax.broadcasted_iota(jnp.int32, (EDGES, EDGES), 1)
    chosen = (dst[...] == atom) & (slot < live_in[0])
    selector = jnp.where(chosen, 1.0, 0.0).astype(BF16)
    load_c.wait()
    edge_cot[0] = tn_dot(selector, node_cot[...]).astype(BF16)
    load_f.wait()

    pl.semaphore_wait(barrier, 2 + (NZ - 1) + (NG - 1))

    feats_copy = shard_copy(feats.at[0], feats.at[1], ex_s.at[0], ex_r.at[0], core_peer)
    cot_copy = shard_copy(edge_cot.at[0], edge_cot.at[1], ex_s.at[1], ex_r.at[1], core_peer)
    feats_copy.start()
    cot_copy.start()

    def fz(off):
        to = ahead(off)
        return shard_copy(merged_send.at[to], block.at[z, q], fz_s, fz_r.at[GROUP_OF[off]], to * NQ + q)

    for off in OFFS[:FAR]:
        fz(off).start()
    for off in range(1, NG):
        dp_copy(coef_all.at[g], coef_all.at[g], co_s, co_r, (g + off) % NG).start()

    feats_copy.wait_recv()
    cot_copy.wait_recv()
    left, right = [], []
    for device in range(2):
        f, c = feats[device], edge_cot[device]
        left += [f[:, :half], f[:, half:]]
        right += [
            jnp.concatenate([c[:, :half], c[:, half:]], axis=1),
            jnp.concatenate([c[:, half:], -c[:, :half]], axis=1),
        ]
    outer = tn_dot(jnp.concatenate(left, axis=0), jnp.concatenate(right, axis=0)) * (1.0 / EDGES)
    grads[0 : NZ // 2] = outer[:, :half].reshape(NZ // 2, 2, 2, ROWS, COLS)
    grads[NZ // 2 : NZ] = outer[:, half:].reshape(NZ // 2, 2, 2, ROWS, COLS)

    def ys(chunk):
        at = pl.ds(chunk * PER, PER)
        return shard_copy(y_send.at[at], y_recv.at[at], ys_s.at[chunk], ys_r.at[chunk], y_peer)

    for chunk in range(YC):
        for j in range(chunk * PER, chunk * PER + PER):
            y_send[j] = grads[ahead(OFFS[j]), 1 - yh, core].astype(BF16)
        ys(chunk).start()

    for chunk in range(YC):
        ys(chunk).wait_recv()
        for j in range(chunk * PER, chunk * PER + PER):
            to = ahead(OFFS[j])
            z_send[j] = (grads[to, yh, core] + y_recv[j].astype(F32)).astype(BF16)
            if j < NZ - 1:
                shard_copy(z_send.at[j], z_recv.at[j], bz_s, bz_r.at[j // 8], to * NQ + q).start()
    z_recv[NZ - 1] = z_send[NZ - 1]

    for off in OFFS[FAR:-1]:
        fz(off).start()

    def forward(group):
        away = [off for off in GROUPS[group] if off > 0]
        arrived(merged_send.at[pl.ds(0, len(away))], fz_r.at[group])
        for off in GROUPS[group]:
            piece = block.at[behind(off), q]
            shard_copy(piece, piece, fy_s, fy_r.at[group], y_peer).start()
            shard_copy(piece, piece, fc_s, fc_r, core_peer).start()

    def forward_again(group):
        arrived(merged_send.at[pl.ds(0, len(GROUPS[group]))], fy_r.at[group])
        for off in GROUPS[group]:
            piece = block.at[behind(off), q_y]
            shard_copy(piece, piece, gc_s, gc_r, core_peer).start()

    def own_slice(group):
        slots = slice(group * 8, group * 8 + 8)
        wide = z_recv[slots].astype(F32)
        z_wide[slots] = wide
        flat = jnp.concatenate([z_wide[slots, row, :] for row in range(ROWS)], axis=1).astype(BF16)
        found = nt_dot(flat, copies[...])
        for j in range(8):
            planes[pl.ds(behind(OFFS[group * 8 + j]), 1), :] = jnp.concatenate([found[j : j + 1], blank], axis=1)
        for to in range(NG):
            rows = slice((to // NX) * 8, (to // NX) * 8 + 8)
            lanes = slice((to % NX) * 128, (to % NX) * 128 + 128)
            for m in range(4):
                dp_send[group, to, m] = jnp.concatenate(
                    [wide[2 * m, rows, lanes], wide[2 * m + 1, rows, lanes]], axis=0
                ).astype(BF16)
        for off in range(1, NG):
            to = (g + off) % NG
            dp_copy(dp_send.at[group, to], dp_recv.at[group, g], da_s.at[group], da_r.at[group], to).start()
        dp_recv[group, g] = dp_send[group, g]

    forward(0)
    arrived(z_recv.at[pl.ds(0, 8)], bz_r.at[0])
    own_slice(0)
    arrived(z_recv.at[pl.ds(0, 7)], bz_r.at[1])
    own_slice(1)

    part[0] = jnp.concatenate([planes[pl.ds(b, 4, stride=4), :][:, :EXPERTS] for b in range(4)], axis=1)
    core_part = shard_copy(part.at[0], part.at[1], pt_s.at[0], pt_r.at[0], core_peer)
    core_part.start()
    core_part.wait_recv()
    part[2] = part[0] + part[1]
    y_part = shard_copy(part.at[2], part.at[3], pt_s.at[1], pt_r.at[1], y_peer)
    y_part.start()

    for group in range(1, len(GROUPS)):
        forward(group)

    y_part.wait_recv()
    sum_send[...] = part[2] + part[3]
    for off in OFFS[:-1]:
        shard_copy(sum_send, sum_recv.at[z], cz_s, cz_r, ahead(off) * NQ + q).start()
    sum_recv[z] = sum_send[...]

    arrived(coef_all.at[pl.ds(0, NG - 1)], co_r)
    all_coef = jnp.concatenate(
        [coef_all[:, 0:8, :].reshape(64, 128), coef_all[:, 8:16, :].reshape(64, 128)], axis=0
    )[:, :EXPERTS]
    all_parts = jnp.concatenate(three_parts(all_coef), axis=1)
    for group in range(2):
        arrived(dp_recv.at[group, pl.ds(0, NG - 1)], da_r.at[group])
    crystals[...] = dp_recv[...].astype(F32).reshape(NZ * NG, 8, 128)
    flat = jnp.concatenate([crystals[:, row, :] for row in range(8)], axis=1).astype(BF16)
    terms = tn_dot(all_parts, flat)
    total = (terms[:EXPERTS] + terms[EXPERTS : 2 * EXPERTS] + terms[2 * EXPERTS :]).astype(BF16)
    for row in range(8):
        gather_send[row] = total[:, row * 128 : row * 128 + 128]
    for off in range(1, NG):
        dp_copy(gather_send, gather.at[pl.ds(h * 8, 8), x], ag_s, ag_r, (g + off) % NG).start()
    gather[pl.ds(h * 8, 8), x] = gather_send[...]

    for group in range(len(GROUPS)):
        forward_again(group)
    arrived(merged_send, fc_r)
    arrived(merged_send, gc_r)

    matrix = block[...].reshape(NZ * NQ * ROWS, COLS)
    f = feats[0]
    lifted = jnp.concatenate(
        [
            jnp.concatenate([f[:, :half], -f[:, half:]], axis=1),
            jnp.concatenate([f[:, half:], f[:, :half]], axis=1),
        ],
        axis=0,
    )
    messages = jnp.dot(lifted, matrix, preferred_element_type=F32).astype(BF16)
    messages = jnp.concatenate([messages[:EDGES], messages[EDGES:]], axis=1)
    node_rows[...] = jnp.dot(selector, messages, preferred_element_type=F32).astype(BF16)
    store_n = pltpu.make_async_copy(node_rows, node_out, out_sem.at[0])
    store_n.start()
    c = edge_cot[0]
    products = nt_dot(jnp.concatenate([c[:, :half], c[:, half:]], axis=0), matrix)
    grad_rows[:, :half] = (products[:EDGES, :half] + products[EDGES:, half:]).astype(BF16)
    grad_rows[:, half:] = (products[EDGES:, :half] - products[:EDGES, half:]).astype(BF16)
    store_e = pltpu.make_async_copy(grad_rows, edge_grad, out_sem.at[1])
    store_e.start()

    arrived(gather.at[pl.ds(0, 14)], ag_r)
    for row in range(ROWS):
        for tile in range(NX):
            weight_rows[:, pl.ds((row * NX + tile) * 128, 128)] = gather[row, tile]
    store_w = pltpu.make_async_copy(weight_rows, weight_out, out_sem.at[2])
    store_w.start()

    arrived(sum_recv.at[pl.ds(0, NZ - 1)], cz_r)
    summed = jnp.sum(sum_recv[...], axis=0)
    coef_out[...] = jnp.concatenate(
        [summed[a : a + 1, b * EXPERTS : (b + 1) * EXPERTS] for a in range(4) for b in range(4)], axis=0
    )

    sent(merged_send.at[pl.ds(0, NZ - 1)], fz_s)
    sent(merged_send, fy_s)
    sent(merged_send, fc_s)
    sent(merged_send, gc_s)
    sent(coef_all.at[pl.ds(0, NG - 1)], co_s)
    sent(z_send.at[pl.ds(0, NZ - 1)], bz_s)
    for group in range(2):
        sent(dp_send.at[group, pl.ds(0, NG - 1)], da_s.at[group])
    sent(gather.at[pl.ds(0, 14)], ag_s)
    sent(sum_recv.at[pl.ds(0, NZ - 1)], cz_s)
    feats_copy.wait_send()
    cot_copy.wait_send()
    core_part.wait_send()
    y_part.wait_send()
    for chunk in range(YC):
        ys(chunk).wait_send()
    store_n.wait()
    store_e.wait()
    store_w.wait()


def per_device(edge_feats, edge_dst, edge_live, coefficients, expert_weights, node_cot):
    vmem = pl.BlockSpec(memory_space=pltpu.VMEM)
    smem = pl.BlockSpec(memory_space=pltpu.SMEM)
    hbm = pl.BlockSpec(memory_space=pl.ANY)
    node_out, edge_grad, weight_grad, coef_grad = pl.pallas_call(
        kernel,
        out_shape=(
            jax.ShapeDtypeStruct((EDGES, WIDTH), BF16),
            jax.ShapeDtypeStruct((EDGES, WIDTH), BF16),
            jax.ShapeDtypeStruct((EXPERTS, ROWS * COLS), BF16),
            jax.ShapeDtypeStruct((NZ, EXPERTS), F32),
        ),
        in_specs=[hbm, hbm, smem, hbm, hbm, hbm],
        out_specs=(hbm, hbm, hbm, vmem),
        scratch_shapes=[
            pltpu.VMEM((EXPERTS, ROWS * COLS), F32),
            pltpu.VMEM((EXPERTS, ROWS * COLS), BF16),
            pltpu.VMEM((NZ, EXPERTS), F32),
            pltpu.VMEM((1, EDGES), jnp.int32),
            pltpu.VMEM((NZ, ROWS, COLS), F32),
            pltpu.VMEM((NZ, ROWS, COLS), BF16),
            pltpu.VMEM((NZ, NQ, ROWS, COLS), BF16),
            pltpu.VMEM((2, EDGES, WIDTH), BF16),
            pltpu.VMEM((EDGES, WIDTH), BF16),
            pltpu.VMEM((2, EDGES, WIDTH), BF16),
            pltpu.VMEM((NZ, 2, 2, ROWS, COLS), F32),
            pltpu.VMEM((NZ, ROWS, COLS), BF16),
            pltpu.VMEM((NZ, ROWS, COLS), BF16),
            pltpu.VMEM((NZ, ROWS, COLS), BF16),
            pltpu.VMEM((NZ, ROWS, COLS), BF16),
            pltpu.VMEM((NZ, ROWS, COLS), F32),
            pltpu.VMEM((2, NG, 4, 16, 128), BF16),
            pltpu.VMEM((2, NG, 4, 16, 128), BF16),
            pltpu.VMEM((NZ * NG, 8, 128), F32),
            pltpu.VMEM((ROWS, NX, EXPERTS, 128), BF16),
            pltpu.VMEM((8, EXPERTS, 128), BF16),
            pltpu.VMEM((NG, NZ, 128), F32),
            pltpu.VMEM((NZ, 128), F32),
            pltpu.VMEM((4, 4, 128), F32),
            pltpu.VMEM((4, 128), F32),
            pltpu.VMEM((NZ, 4, 128), F32),
            pltpu.VMEM((EDGES, WIDTH), BF16),
            pltpu.VMEM((EDGES, WIDTH), BF16),
            pltpu.VMEM((EXPERTS, ROWS * COLS), BF16),
            DMA((5,)), DMA((3,)),
            DMA, DMA((len(GROUPS),)), DMA, DMA((len(GROUPS),)), DMA, DMA, DMA, DMA,
            DMA((2,)), DMA((2,)), DMA, DMA,
            DMA((YC,)), DMA((YC,)), DMA, DMA((2,)), DMA((2,)), DMA((2,)),
            DMA, DMA, DMA, DMA, DMA((2,)), DMA((2,)),
        ],
        compiler_params=pltpu.CompilerParams(
            collective_id=0, has_side_effects=True, vmem_limit_bytes=60 * 1024 * 1024
        ),
    )(edge_feats, edge_dst.reshape(1, EDGES), edge_live, coefficients, expert_weights, node_cot)
    return node_out, edge_grad, weight_grad.astype(F32), coef_grad


def solution(mesh):
    in_specs = (
        P(("dp", "shard"), None),
        P(("dp", "shard")),
        P(("dp", "shard")),
        P("dp", None),
        P(None, "shard"),
        P(("dp", "shard"), None),
    )
    out_specs = (
        P(("dp", "shard"), None),
        P(("dp", "shard"), None),
        P(None, "shard"),
        P("dp", None),
    )
    return jax.shard_map(
        per_device, mesh=mesh, in_specs=in_specs, out_specs=out_specs, check_vma=False
    )
```

```python
import jax
import jax.numpy as jnp
from jax import lax
from jax.experimental import pallas as pl
from jax.experimental.pallas import tpu as pltpu
from jax.sharding import PartitionSpec as P

F32, BF16 = jnp.float32, jnp.bfloat16
NZ, NQ, NG = 16, 4, 8
NX = 4
ROWS, COLS = 16, 512
EDGES, WIDTH, EXPERTS = 128, 1024, 32
YC = 4
PER = NZ // YC
OFFS = [8, 7, 9, 6, 10, 5, 11, 4, 12, 3, 13, 2, 14, 1, 15, 0]
FIRST, SECOND, THIRD = [4, 12, 3, 13, 2, 14, 1, 15], [8, 7, 9], [6, 10, 5, 11]
GROUPS = [[0, 4, 12, 3, 13, 2, 14, 1, 15], [8, 7, 9], [6, 10], [5, 11]]
NEAR = [4, 12, 3, 13, 2, 14, 1, 15]
PARTS = 4
FINISH_LIMIT = 60
GROUP_OF = {off: group for group, offs in enumerate(GROUPS) for off in offs}
DMA = pltpu.SemaphoreType.DMA


def three_parts(value):
    high = value.astype(BF16)
    rest = value - high.astype(F32)
    middle = rest.astype(BF16)
    low = (rest - middle.astype(F32)).astype(BF16)
    return high, middle, low


def tn_dot(a, b):
    return lax.dot_general(a, b, (((0,), (0,)), ((), ())), preferred_element_type=F32)


def nt_dot(a, b):
    return lax.dot_general(a, b, (((1,), (1,)), ((), ())), preferred_element_type=F32)


def kernel(
    feats_in, dst_in, live_in, coef_in, weights_in, cot_in,
    node_out, edge_grad, weight_out, coef_out,
    weights, copies, coef, dst, merged_rows, merged_send, block, feats, node_cot, edge_cot,
    grads, y_send, y_recv, z_send, z_recv, z_wide, dp_send, dp_recv, crystals, gather,
    gather_send, coef_all, planes, part, sum_send, sum_recv,
    node_rows, grad_rows,
    in_sem, out_sem, fz_s, fz_r, fy_s, fy_r, fc_s, fc_r, gc_s, gc_r, ex_s, ex_r, co_s, co_r,
    ys_s, ys_r, bz_s, bz_r, da_s, da_r, ag_s, ag_r, ah_s, ah_r, cz_s, cz_r, pt_s, pt_r, far_sem,
):
    g = lax.axis_index("dp")
    s = lax.axis_index("shard")
    z = s // NQ
    q = s % NQ
    yh = q // 2
    core = q % 2
    h = g // NX
    x = g % NX
    q_y = (1 - yh) * 2 + core
    q_c = yh * 2 + (1 - core)
    q_yc = (1 - yh) * 2 + (1 - core)
    core_peer = z * NQ + q_c
    y_peer = z * NQ + q_y
    half = WIDTH // 2

    load_w = pltpu.make_async_copy(weights_in, weights, in_sem.at[0])
    load_f = pltpu.make_async_copy(feats_in, feats.at[0], in_sem.at[1])
    load_c = pltpu.make_async_copy(cot_in, node_cot, in_sem.at[2])
    load_k = pltpu.make_async_copy(coef_in, coef, in_sem.at[3])
    load_d = pltpu.make_async_copy(dst_in, dst, in_sem.at[4])
    for load in (load_w, load_k, load_d, load_c, load_f):
        load.start()

    def copy_to(src, dst, send, recv, dp, shard):
        return pltpu.make_async_remote_copy(
            src_ref=src, dst_ref=dst, send_sem=send, recv_sem=recv,
            device_id={"dp": dp, "shard": shard}, device_id_type=pl.DeviceIdType.MESH,
        )

    def shard_copy(src, dst, send, recv, peer):
        return copy_to(src, dst, send, recv, g, peer)

    def dp_copy(src, dst, send, recv, peer):
        return copy_to(src, dst, send, recv, peer, s)

    def sent(ref, sem):
        shard_copy(ref, ref, sem, sem, core_peer).wait_send()

    def arrived(ref, sem):
        shard_copy(ref, ref, sem, sem, core_peer).wait_recv()

    def ahead(off):
        return (z + off) % NZ

    def behind(off):
        return (z + NZ - off) % NZ

    barrier = pltpu.get_barrier_semaphore()

    def greet(dp, shard):
        pl.semaphore_signal(
            barrier, inc=1, device_id={"dp": dp, "shard": shard}, device_id_type=pl.DeviceIdType.MESH
        )

    for off in NEAR:
        greet(g, ahead(off) * NQ + q)
    for off in range(1, NG):
        greet((g + off) % NG, s)
    greet(g, core_peer)
    greet(g, y_peer)

    load_k.wait()
    stacked = jnp.concatenate(three_parts(coef[...]), axis=0)
    blank = jnp.zeros((1, 128 - EXPERTS), F32)
    for j in range(NZ):
        row = coef[pl.ds(behind(OFFS[j]), 1), :]
        coef_all[g, pl.ds(j, 1), :] = jnp.concatenate([row, blank], axis=1)
    load_w.wait()
    for row in range(ROWS):
        lanes = pl.ds(row * COLS, COLS)
        rounded = weights[:, lanes].astype(BF16)
        copies[:, lanes] = rounded
        terms = jnp.dot(stacked, rounded, preferred_element_type=F32)
        merged_rows[:, row, :] = terms[0:NZ] + terms[NZ : 2 * NZ] + terms[2 * NZ : 3 * NZ]
    merged_send[...] = merged_rows[...].astype(BF16)
    block[z, q] = merged_send[z]

    load_d.wait()
    atom = lax.broadcasted_iota(jnp.int32, (EDGES, EDGES), 0)
    slot = lax.broadcasted_iota(jnp.int32, (EDGES, EDGES), 1)
    chosen = (dst[...] == atom) & (slot < live_in[0])
    selector = jnp.where(chosen, 1.0, 0.0).astype(BF16)
    load_c.wait()
    edge_cot[0] = tn_dot(selector, node_cot[...]).astype(BF16)
    load_f.wait()

    pl.semaphore_wait(barrier, 2 + len(NEAR) + (NG - 1))
    for off in (4, NZ - 4):
        pl.semaphore_signal(
            far_sem, inc=1, device_id={"dp": g, "shard": ahead(off) * NQ + q}, device_id_type=pl.DeviceIdType.MESH
        )

    feats_copy = shard_copy(feats.at[0], feats.at[1], ex_s.at[0], ex_r.at[0], core_peer)
    cot_copy = shard_copy(edge_cot.at[0], edge_cot.at[1], ex_s.at[1], ex_r.at[1], core_peer)
    feats_copy.start()
    cot_copy.start()

    def fz(off):
        to = ahead(off)
        return shard_copy(merged_send.at[to], block.at[z, q], fz_s, fz_r.at[GROUP_OF[off]], to * NQ + q)

    for off in FIRST:
        fz(off).start()
    for off in range(1, NG):
        dp_copy(coef_all.at[g], coef_all.at[g], co_s, co_r, (g + off) % NG).start()

    feats_copy.wait_recv()
    cot_copy.wait_recv()
    left, right = [], []
    for device in range(2):
        f, c = feats[device], edge_cot[device]
        left += [f[:, :half], f[:, half:]]
        right += [
            jnp.concatenate([c[:, :half], c[:, half:]], axis=1),
            jnp.concatenate([c[:, half:], -c[:, :half]], axis=1),
        ]
    outer = tn_dot(jnp.concatenate(left, axis=0), jnp.concatenate(right, axis=0)) * (1.0 / EDGES)
    grads[0 : NZ // 2] = outer[:, :half].reshape(NZ // 2, 2, 2, ROWS, COLS)
    grads[NZ // 2 : NZ] = outer[:, half:].reshape(NZ // 2, 2, 2, ROWS, COLS)

    def ys(chunk):
        at = pl.ds(chunk * PER, PER)
        return shard_copy(y_send.at[at], y_recv.at[at], ys_s.at[chunk], ys_r.at[chunk], y_peer)

    for chunk in range(YC):
        for j in range(chunk * PER, chunk * PER + PER):
            y_send[j] = grads[ahead(OFFS[j]), 1 - yh, core].astype(BF16)
        ys(chunk).start()

    pl.semaphore_wait(far_sem, 2)
    for off in SECOND:
        fz(off).start()

    for chunk in range(YC):
        ys(chunk).wait_recv()
        for j in range(chunk * PER, chunk * PER + PER):
            to = ahead(OFFS[j])
            z_send[j] = (grads[to, yh, core] + y_recv[j].astype(F32)).astype(BF16)
            if j < NZ - 1:
                shard_copy(z_send.at[j], z_recv.at[j], bz_s, bz_r.at[j // 8], to * NQ + q).start()
    z_recv[NZ - 1] = z_send[NZ - 1]

    for off in THIRD:
        fz(off).start()

    def forward(group):
        away = [off for off in GROUPS[group] if off > 0]
        arrived(merged_send.at[pl.ds(0, len(away))], fz_r.at[group])
        for off in GROUPS[group]:
            piece = block.at[behind(off), q]
            shard_copy(piece, piece, fy_s, fy_r.at[group], y_peer).start()
            shard_copy(piece, piece, fc_s, fc_r, core_peer).start()

    def forward_again(group):
        arrived(merged_send.at[pl.ds(0, len(GROUPS[group]))], fy_r.at[group])
        for off in GROUPS[group]:
            piece = block.at[behind(off), q_y]
            shard_copy(piece, piece, gc_s, gc_r, core_peer).start()

    def own_slice(group):
        slots = slice(group * 8, group * 8 + 8)
        wide = z_recv[slots].astype(F32)
        z_wide[slots] = wide
        flat = jnp.concatenate([z_wide[slots, row, :] for row in range(ROWS)], axis=1).astype(BF16)
        found = nt_dot(flat, copies[...])
        for j in range(8):
            planes[pl.ds(behind(OFFS[group * 8 + j]), 1), :] = jnp.concatenate([found[j : j + 1], blank], axis=1)
        for to in range(NG):
            rows = slice((to // NX) * 8, (to // NX) * 8 + 8)
            lanes = slice((to % NX) * 128, (to % NX) * 128 + 128)
            for m in range(4):
                dp_send[group, to, m] = jnp.concatenate(
                    [wide[2 * m, rows, lanes], wide[2 * m + 1, rows, lanes]], axis=0
                ).astype(BF16)
        for off in range(1, NG):
            to = (g + off) % NG
            dp_copy(dp_send.at[group, to], dp_recv.at[group, g], da_s.at[group], da_r.at[group], to).start()
        dp_recv[group, g] = dp_send[group, g]

    forward(0)
    arrived(z_recv.at[pl.ds(0, 8)], bz_r.at[0])
    own_slice(0)
    arrived(z_recv.at[pl.ds(0, 7)], bz_r.at[1])
    own_slice(1)

    part[0] = jnp.concatenate([planes[pl.ds(b, 4, stride=4), :][:, :EXPERTS] for b in range(4)], axis=1)
    core_part = shard_copy(part.at[0], part.at[1], pt_s.at[0], pt_r.at[0], core_peer)
    core_part.start()
    core_part.wait_recv()
    part[2] = part[0] + part[1]
    y_part = shard_copy(part.at[2], part.at[3], pt_s.at[1], pt_r.at[1], y_peer)
    y_part.start()

    for group in range(1, len(GROUPS)):
        forward(group)

    y_part.wait_recv()
    sum_send[...] = part[2] + part[3]
    for off in OFFS[:-1]:
        shard_copy(sum_send, sum_recv.at[z], cz_s, cz_r, ahead(off) * NQ + q).start()
    sum_recv[z] = sum_send[...]

    arrived(coef_all.at[pl.ds(0, NG - 1)], co_r)
    all_coef = jnp.concatenate(
        [coef_all[:, 0:8, :].reshape(64, 128), coef_all[:, 8:16, :].reshape(64, 128)], axis=0
    )[:, :EXPERTS]
    all_parts = jnp.concatenate(three_parts(all_coef), axis=1)
    for group in range(2):
        arrived(dp_recv.at[group, pl.ds(0, NG - 1)], da_r.at[group])
    crystals[...] = dp_recv[...].astype(F32).reshape(NZ * NG, 8, 128)
    flat = jnp.concatenate([crystals[:, row, :] for row in range(8)], axis=1).astype(BF16)
    terms = tn_dot(all_parts, flat)
    total = (terms[:EXPERTS] + terms[EXPERTS : 2 * EXPERTS] + terms[2 * EXPERTS :]).astype(BF16)
    for row in range(8):
        gather_send[row] = total[:, row * 128 : row * 128 + 128]
    own_rows = pl.ds(h * 8, 8)
    other_rows = pl.ds((1 - h) * 8, 8)
    dp_copy(gather_send, gather.at[own_rows, x], ah_s, ah_r, (1 - h) * NX + x).start()
    for off in (2, 1, 3):
        dp_copy(gather_send, gather.at[own_rows, x], ag_s, ag_r, h * NX + (x + off) % NX).start()
    gather[pl.ds(h * 8, 8), x] = gather_send[...]

    arrived(gather_send, ah_r)
    relayed = gather.at[other_rows, x]
    for off in (2, 1, 3):
        dp_copy(relayed, relayed, ag_s, ag_r, h * NX + (x + off) % NX).start()
    for group in range(len(GROUPS)):
        forward_again(group)
    arrived(merged_send, fc_r)
    arrived(merged_send, gc_r)

    matrix = block[...].reshape(NZ * NQ * ROWS, COLS)
    f = feats[0]
    lifted = jnp.concatenate(
        [
            jnp.concatenate([f[:, :half], -f[:, half:]], axis=1),
            jnp.concatenate([f[:, half:], f[:, :half]], axis=1),
        ],
        axis=0,
    )
    messages = jnp.dot(lifted, matrix, preferred_element_type=F32).astype(BF16)
    messages = jnp.concatenate([messages[:EDGES], messages[EDGES:]], axis=1)
    node_rows[...] = jnp.dot(selector, messages, preferred_element_type=F32).astype(BF16)
    store_n = pltpu.make_async_copy(node_rows, node_out, out_sem.at[0])
    store_n.start()
    c = edge_cot[0]
    products = nt_dot(jnp.concatenate([c[:, :half], c[:, half:]], axis=0), matrix)
    grad_rows[:, :half] = (products[:EDGES, :half] + products[EDGES:, half:]).astype(BF16)
    grad_rows[:, half:] = (products[EDGES:, :half] - products[:EDGES, half:]).astype(BF16)
    store_e = pltpu.make_async_copy(grad_rows, edge_grad, out_sem.at[1])
    store_e.start()

    arrived(gather.at[pl.ds(0, 12)], ag_r)
    store_w = pltpu.make_async_copy(gather, weight_out, out_sem.at[2])
    store_w.start()

    arrived(sum_recv.at[pl.ds(0, NZ - 1)], cz_r)
    summed = jnp.sum(sum_recv[...], axis=0)
    coef_out[...] = jnp.concatenate(
        [summed[a : a + 1, b * EXPERTS : (b + 1) * EXPERTS] for a in range(4) for b in range(4)], axis=0
    )

    sent(merged_send.at[pl.ds(0, NZ - 1)], fz_s)
    sent(merged_send, fy_s)
    sent(merged_send, fc_s)
    sent(merged_send, gc_s)
    sent(coef_all.at[pl.ds(0, NG - 1)], co_s)
    sent(z_send.at[pl.ds(0, NZ - 1)], bz_s)
    for group in range(2):
        sent(dp_send.at[group, pl.ds(0, NG - 1)], da_s.at[group])
    sent(gather.at[pl.ds(0, 12)], ag_s)
    sent(gather_send, ah_s)
    sent(sum_recv.at[pl.ds(0, NZ - 1)], cz_s)
    feats_copy.wait_send()
    cot_copy.wait_send()
    core_part.wait_send()
    y_part.wait_send()
    for chunk in range(YC):
        ys(chunk).wait_send()
    store_n.wait()
    store_e.wait()
    store_w.wait()


def finish(
    node_rows, grad_rows, gathered, coef_rows, node_out, edge_grad, weight_out, coef_out,
    tiles, wide, node_held, grad_held, coef_held, sem, in_sem, out_sem,
):
    per = ROWS // PARTS
    moves = [
        (pltpu.make_async_copy(src, held, sem.at[n]), pltpu.make_async_copy(held, dst, sem.at[3 + n]))
        for n, (src, held, dst) in enumerate(
            ((node_rows, node_held, node_out), (grad_rows, grad_held, edge_grad), (coef_rows, coef_held, coef_out))
        )
    ]
    loads = [
        pltpu.make_async_copy(gathered.at[pl.ds(n * per, per)], tiles.at[pl.ds(n * per, per)], in_sem.at[n])
        for n in range(PARTS)
    ]
    for load in loads:
        load.start()
    for load, _ in moves:
        load.start()
    stores = []
    for n in range(PARTS):
        loads[n].wait()
        for row in range(n * per, n * per + per):
            for tile in range(NX):
                wide[:, pl.ds((row * NX + tile) * 128, 128)] = tiles[row, tile].astype(F32)
        lanes = pl.ds(n * per * COLS, per * COLS)
        stores.append(pltpu.make_async_copy(wide.at[:, lanes], weight_out.at[:, lanes], out_sem.at[n]))
        stores[n].start()
    for load, store in moves:
        load.wait()
        store.start()
    for store in [store for _, store in moves] + stores:
        store.wait()


def per_device(edge_feats, edge_dst, edge_live, coefficients, expert_weights, node_cot):
    vmem = pl.BlockSpec(memory_space=pltpu.VMEM)
    smem = pl.BlockSpec(memory_space=pltpu.SMEM)
    hbm = pl.BlockSpec(memory_space=pl.ANY)
    node_rows, grad_rows, gathered, coef_rows = pl.pallas_call(
        kernel,
        out_shape=(
            jax.ShapeDtypeStruct((EDGES, WIDTH), BF16),
            jax.ShapeDtypeStruct((EDGES, WIDTH), BF16),
            jax.ShapeDtypeStruct((ROWS, NX, EXPERTS, 128), BF16),
            jax.ShapeDtypeStruct((NZ, EXPERTS), F32),
        ),
        in_specs=[hbm, hbm, smem, hbm, hbm, hbm],
        out_specs=(hbm, hbm, hbm, vmem),
        scratch_shapes=[
            pltpu.VMEM((EXPERTS, ROWS * COLS), F32),
            pltpu.VMEM((EXPERTS, ROWS * COLS), BF16),
            pltpu.VMEM((NZ, EXPERTS), F32),
            pltpu.VMEM((1, EDGES), jnp.int32),
            pltpu.VMEM((NZ, ROWS, COLS), F32),
            pltpu.VMEM((NZ, ROWS, COLS), BF16),
            pltpu.VMEM((NZ, NQ, ROWS, COLS), BF16),
            pltpu.VMEM((2, EDGES, WIDTH), BF16),
            pltpu.VMEM((EDGES, WIDTH), BF16),
            pltpu.VMEM((2, EDGES, WIDTH), BF16),
            pltpu.VMEM((NZ, 2, 2, ROWS, COLS), F32),
            pltpu.VMEM((NZ, ROWS, COLS), BF16),
            pltpu.VMEM((NZ, ROWS, COLS), BF16),
            pltpu.VMEM((NZ, ROWS, COLS), BF16),
            pltpu.VMEM((NZ, ROWS, COLS), BF16),
            pltpu.VMEM((NZ, ROWS, COLS), F32),
            pltpu.VMEM((2, NG, 4, 16, 128), BF16),
            pltpu.VMEM((2, NG, 4, 16, 128), BF16),
            pltpu.VMEM((NZ * NG, 8, 128), F32),
            pltpu.VMEM((ROWS, NX, EXPERTS, 128), BF16),
            pltpu.VMEM((8, EXPERTS, 128), BF16),
            pltpu.VMEM((NG, NZ, 128), F32),
            pltpu.VMEM((NZ, 128), F32),
            pltpu.VMEM((4, 4, 128), F32),
            pltpu.VMEM((4, 128), F32),
            pltpu.VMEM((NZ, 4, 128), F32),
            pltpu.VMEM((EDGES, WIDTH), BF16),
            pltpu.VMEM((EDGES, WIDTH), BF16),
            DMA((5,)), DMA((3,)),
            DMA, DMA((len(GROUPS),)), DMA, DMA((len(GROUPS),)), DMA, DMA, DMA, DMA,
            DMA((2,)), DMA((2,)), DMA, DMA,
            DMA((YC,)), DMA((YC,)), DMA, DMA((2,)), DMA((2,)), DMA((2,)),
            DMA, DMA, DMA, DMA, DMA, DMA, DMA((2,)), DMA((2,)), pltpu.SemaphoreType.REGULAR,
        ],
        compiler_params=pltpu.CompilerParams(
            collective_id=0, has_side_effects=True, vmem_limit_bytes=60 * 1024 * 1024
        ),
    )(edge_feats, edge_dst.reshape(1, EDGES), edge_live, coefficients, expert_weights, node_cot)
    return pl.pallas_call(
        finish,
        out_shape=(
            jax.ShapeDtypeStruct((EDGES, WIDTH), BF16),
            jax.ShapeDtypeStruct((EDGES, WIDTH), BF16),
            jax.ShapeDtypeStruct((EXPERTS, ROWS * COLS), F32),
            jax.ShapeDtypeStruct((NZ, EXPERTS), F32),
        ),
        in_specs=[hbm, hbm, hbm, hbm],
        out_specs=(hbm, hbm, hbm, hbm),
        scratch_shapes=[
            pltpu.VMEM((ROWS, NX, EXPERTS, 128), BF16),
            pltpu.VMEM((EXPERTS, ROWS * COLS), F32),
            pltpu.VMEM((EDGES, WIDTH), BF16),
            pltpu.VMEM((EDGES, WIDTH), BF16),
            pltpu.VMEM((NZ, EXPERTS), F32),
            DMA((6,)), DMA((PARTS,)), DMA((PARTS,)),
        ],
        compiler_params=pltpu.CompilerParams(vmem_limit_bytes=FINISH_LIMIT * 1024 * 1024),
    )(node_rows, grad_rows, gathered, coef_rows)


def solution(mesh):
    in_specs = (
        P(("dp", "shard"), None),
        P(("dp", "shard")),
        P(("dp", "shard")),
        P("dp", None),
        P(None, "shard"),
        P(("dp", "shard"), None),
    )
    out_specs = (
        P(("dp", "shard"), None),
        P(("dp", "shard"), None),
        P(None, "shard"),
        P("dp", None),
    )
    return jax.shard_map(
        per_device, mesh=mesh, in_specs=in_specs, out_specs=out_specs, check_vma=False
    )
```

```python
import jax
import jax.numpy as jnp
from jax import lax
from jax.experimental import pallas as pl
from jax.experimental.pallas import tpu as pltpu
from jax.sharding import PartitionSpec as P

F32, BF16 = jnp.float32, jnp.bfloat16
NZ, NQ, NG = 16, 4, 8
NX = 4
ROWS, COLS = 16, 512
EDGES, WIDTH, EXPERTS = 128, 1024, 32
YC = 4
PER = NZ // YC
OFFS = [8, 7, 9, 6, 10, 5, 11, 4, 12, 3, 13, 2, 14, 1, 15, 0]
FIRST, SECOND, THIRD = [4, 12, 3, 13, 2, 14, 1, 15], [8, 7, 9], [6, 10, 5, 11]
GROUPS = [[0, 4, 12, 3, 13, 2, 14, 1, 15], [8, 7, 9], [6, 10], [5, 11]]
NEAR = [4, 12, 3, 13, 2, 14, 1, 15]
PARTS = 4
FINISH_LIMIT = 60
GROUP_OF = {off: group for group, offs in enumerate(GROUPS) for off in offs}
DMA = pltpu.SemaphoreType.DMA


def three_parts(value):
    high = value.astype(BF16)
    rest = value - high.astype(F32)
    middle = rest.astype(BF16)
    low = (rest - middle.astype(F32)).astype(BF16)
    return high, middle, low


def tn_dot(a, b):
    return lax.dot_general(a, b, (((0,), (0,)), ((), ())), preferred_element_type=F32)


def nt_dot(a, b):
    return lax.dot_general(a, b, (((1,), (1,)), ((), ())), preferred_element_type=F32)


def kernel(
    feats_in, dst_in, live_in, coef_in, weights_in, cot_in,
    node_out, edge_grad, weight_out, coef_out,
    weights, copies, coef, dst, merged_rows, merged_send, block, feats, node_cot, edge_cot,
    grads, y_send, y_recv, z_send, z_recv, z_wide, dp_send, dp_recv, crystals,
    gather_send, coef_all, planes, part, sum_send, sum_recv,
    node_rows, grad_rows,
    in_sem, out_sem, fz_s, fz_r, fy_s, fy_r, fc_s, fc_r, gc_s, gc_r, ex_s, ex_r, co_s, co_r,
    ys_s, ys_r, bz_s, bz_r, da_s, da_r, ag_s, ag_r, cz_s, cz_r, pt_s, pt_r, far_sem,
):
    g = lax.axis_index("dp")
    s = lax.axis_index("shard")
    z = s // NQ
    q = s % NQ
    yh = q // 2
    core = q % 2
    h = g // NX
    x = g % NX
    q_y = (1 - yh) * 2 + core
    q_c = yh * 2 + (1 - core)
    q_yc = (1 - yh) * 2 + (1 - core)
    core_peer = z * NQ + q_c
    y_peer = z * NQ + q_y
    half = WIDTH // 2

    load_w = pltpu.make_async_copy(weights_in, weights, in_sem.at[0])
    load_f = pltpu.make_async_copy(feats_in, feats.at[0], in_sem.at[1])
    load_c = pltpu.make_async_copy(cot_in, node_cot, in_sem.at[2])
    load_k = pltpu.make_async_copy(coef_in, coef, in_sem.at[3])
    load_d = pltpu.make_async_copy(dst_in, dst, in_sem.at[4])
    for load in (load_d, load_c, load_f, load_k, load_w):
        load.start()

    def copy_to(src, dst, send, recv, dp, shard):
        return pltpu.make_async_remote_copy(
            src_ref=src, dst_ref=dst, send_sem=send, recv_sem=recv,
            device_id={"dp": dp, "shard": shard}, device_id_type=pl.DeviceIdType.MESH,
        )

    def shard_copy(src, dst, send, recv, peer):
        return copy_to(src, dst, send, recv, g, peer)

    def dp_copy(src, dst, send, recv, peer):
        return copy_to(src, dst, send, recv, peer, s)

    def sent(ref, sem):
        shard_copy(ref, ref, sem, sem, core_peer).wait_send()

    def arrived(ref, sem):
        shard_copy(ref, ref, sem, sem, core_peer).wait_recv()

    def ahead(off):
        return (z + off) % NZ

    def behind(off):
        return (z + NZ - off) % NZ

    barrier = pltpu.get_barrier_semaphore()

    def greet(dp, shard):
        pl.semaphore_signal(
            barrier, inc=1, device_id={"dp": dp, "shard": shard}, device_id_type=pl.DeviceIdType.MESH
        )

    for off in NEAR:
        greet(g, ahead(off) * NQ + q)
    for off in range(1, NG):
        greet((g + off) % NG, s)
    greet(g, core_peer)
    greet(g, y_peer)

    load_d.wait()
    atom = lax.broadcasted_iota(jnp.int32, (EDGES, EDGES), 0)
    slot = lax.broadcasted_iota(jnp.int32, (EDGES, EDGES), 1)
    chosen = (dst[...] == atom) & (slot < live_in[0])
    selector = jnp.where(chosen, 1.0, 0.0).astype(BF16)
    load_c.wait()
    edge_cot[0] = tn_dot(selector, node_cot[...]).astype(BF16)
    load_f.wait()

    pl.semaphore_wait(barrier, 2 + len(NEAR) + (NG - 1))
    for off in (4, NZ - 4):
        pl.semaphore_signal(
            far_sem, inc=1, device_id={"dp": g, "shard": ahead(off) * NQ + q}, device_id_type=pl.DeviceIdType.MESH
        )

    feats_copy = shard_copy(feats.at[0], feats.at[1], ex_s.at[0], ex_r.at[0], core_peer)
    cot_copy = shard_copy(edge_cot.at[0], edge_cot.at[1], ex_s.at[1], ex_r.at[1], core_peer)
    feats_copy.start()
    cot_copy.start()

    load_k.wait()
    stacked = jnp.concatenate(three_parts(coef[...]), axis=0)
    blank = jnp.zeros((1, 128 - EXPERTS), F32)
    for j in range(NZ):
        row = coef[pl.ds(behind(OFFS[j]), 1), :]
        coef_all[g, pl.ds(j, 1), :] = jnp.concatenate([row, blank], axis=1)
    load_w.wait()
    for row in range(ROWS):
        lanes = pl.ds(row * COLS, COLS)
        rounded = weights[:, lanes].astype(BF16)
        copies[:, lanes] = rounded
        terms = jnp.dot(stacked, rounded, preferred_element_type=F32)
        merged_rows[:, row, :] = terms[0:NZ] + terms[NZ : 2 * NZ] + terms[2 * NZ : 3 * NZ]
    merged_send[...] = merged_rows[...].astype(BF16)
    block[z, q] = merged_send[z]

    def fz(off):
        to = ahead(off)
        return shard_copy(merged_send.at[to], block.at[z, q], fz_s, fz_r.at[GROUP_OF[off]], to * NQ + q)

    for off in FIRST:
        fz(off).start()
    for off in range(1, NG):
        dp_copy(coef_all.at[g], coef_all.at[g], co_s, co_r, (g + off) % NG).start()

    feats_copy.wait_recv()
    cot_copy.wait_recv()
    left, right = [], []
    for device in range(2):
        f, c = feats[device], edge_cot[device]
        left += [f[:, :half], f[:, half:]]
        right += [
            jnp.concatenate([c[:, :half], c[:, half:]], axis=1),
            jnp.concatenate([c[:, half:], -c[:, :half]], axis=1),
        ]
    outer = tn_dot(jnp.concatenate(left, axis=0), jnp.concatenate(right, axis=0)) * (1.0 / EDGES)
    grads[0 : NZ // 2] = outer[:, :half].reshape(NZ // 2, 2, 2, ROWS, COLS)
    grads[NZ // 2 : NZ] = outer[:, half:].reshape(NZ // 2, 2, 2, ROWS, COLS)

    def ys(chunk):
        at = pl.ds(chunk * PER, PER)
        return shard_copy(y_send.at[at], y_recv.at[at], ys_s.at[chunk], ys_r.at[chunk], y_peer)

    for chunk in range(YC):
        for j in range(chunk * PER, chunk * PER + PER):
            y_send[j] = grads[ahead(OFFS[j]), 1 - yh, core].astype(BF16)
        ys(chunk).start()

    pl.semaphore_wait(far_sem, 2)
    for off in SECOND:
        fz(off).start()

    for chunk in range(YC):
        ys(chunk).wait_recv()
        for j in range(chunk * PER, chunk * PER + PER):
            to = ahead(OFFS[j])
            z_send[j] = (grads[to, yh, core] + y_recv[j].astype(F32)).astype(BF16)
            if j < NZ - 1:
                shard_copy(z_send.at[j], z_recv.at[j], bz_s, bz_r.at[j // 8], to * NQ + q).start()
    z_recv[NZ - 1] = z_send[NZ - 1]

    for off in THIRD:
        fz(off).start()

    def forward(group):
        away = [off for off in GROUPS[group] if off > 0]
        arrived(merged_send.at[pl.ds(0, len(away))], fz_r.at[group])
        for off in GROUPS[group]:
            piece = block.at[behind(off), q]
            shard_copy(piece, piece, fy_s, fy_r.at[group], y_peer).start()
            shard_copy(piece, piece, fc_s, fc_r, core_peer).start()

    def forward_again(group):
        arrived(merged_send.at[pl.ds(0, len(GROUPS[group]))], fy_r.at[group])
        for off in GROUPS[group]:
            piece = block.at[behind(off), q_y]
            shard_copy(piece, piece, gc_s, gc_r, core_peer).start()

    def own_slice(group):
        slots = slice(group * 8, group * 8 + 8)
        wide = z_recv[slots].astype(F32)
        z_wide[slots] = wide
        flat = jnp.concatenate([z_wide[slots, row, :] for row in range(ROWS)], axis=1).astype(BF16)
        found = nt_dot(flat, copies[...])
        for j in range(8):
            planes[pl.ds(behind(OFFS[group * 8 + j]), 1), :] = jnp.concatenate([found[j : j + 1], blank], axis=1)
        for to in range(NG):
            rows = slice((to // NX) * 8, (to // NX) * 8 + 8)
            lanes = slice((to % NX) * 128, (to % NX) * 128 + 128)
            for m in range(4):
                dp_send[group, to, m] = jnp.concatenate(
                    [wide[2 * m, rows, lanes], wide[2 * m + 1, rows, lanes]], axis=0
                ).astype(BF16)
        for off in range(1, NG):
            to = (g + off) % NG
            dp_copy(dp_send.at[group, to], dp_recv.at[group, g], da_s.at[group], da_r.at[group], to).start()
        dp_recv[group, g] = dp_send[group, g]

    for group in range(2):
        forward(group)
    arrived(z_recv.at[pl.ds(0, 8)], bz_r.at[0])
    own_slice(0)
    arrived(z_recv.at[pl.ds(0, 7)], bz_r.at[1])
    own_slice(1)

    part[0] = jnp.concatenate([planes[pl.ds(b, 4, stride=4), :][:, :EXPERTS] for b in range(4)], axis=1)
    core_part = shard_copy(part.at[0], part.at[1], pt_s.at[0], pt_r.at[0], core_peer)
    core_part.start()
    core_part.wait_recv()
    part[2] = part[0] + part[1]
    y_part = shard_copy(part.at[2], part.at[3], pt_s.at[1], pt_r.at[1], y_peer)
    y_part.start()

    forward(2)

    forward(3)
    arrived(coef_all.at[pl.ds(0, NG - 1)], co_r)
    all_coef = jnp.concatenate(
        [coef_all[:, 0:8, :].reshape(64, 128), coef_all[:, 8:16, :].reshape(64, 128)], axis=0
    )[:, :EXPERTS]
    all_parts = jnp.concatenate(three_parts(all_coef), axis=1)
    for group in range(2):
        arrived(dp_recv.at[group, pl.ds(0, NG - 1)], da_r.at[group])
    crystals[...] = dp_recv[...].astype(F32).reshape(NZ * NG, 8, 128)
    flat = jnp.concatenate([crystals[:, row, :] for row in range(8)], axis=1).astype(BF16)
    terms = tn_dot(all_parts, flat)
    total = (terms[:EXPERTS] + terms[EXPERTS : 2 * EXPERTS] + terms[2 * EXPERTS :]).astype(BF16)
    for row in range(8):
        gather_send[row] = total[:, row * 128 : row * 128 + 128]
    own_rows = pl.ds(h * 8, 8)
    for off in (6, 2, 5, 7, 1, 3, 4):
        dp_copy(gather_send, weight_out.at[own_rows, x], ag_s, ag_r, (g + off) % NG).start()
    store_w = pltpu.make_async_copy(gather_send, weight_out.at[own_rows, x], out_sem.at[2])
    store_w.start()

    y_part.wait_recv()
    sum_send[...] = part[2] + part[3]
    for off in OFFS[:-1]:
        shard_copy(sum_send, sum_recv.at[z], cz_s, cz_r, ahead(off) * NQ + q).start()
    sum_recv[z] = sum_send[...]

    for group in range(len(GROUPS)):
        forward_again(group)
    arrived(merged_send, fc_r)
    arrived(merged_send, gc_r)

    matrix = block[...].reshape(NZ * NQ * ROWS, COLS)
    f = feats[0]
    lifted = jnp.concatenate(
        [
            jnp.concatenate([f[:, :half], -f[:, half:]], axis=1),
            jnp.concatenate([f[:, half:], f[:, :half]], axis=1),
        ],
        axis=0,
    )
    messages = jnp.dot(lifted, matrix, preferred_element_type=F32).astype(BF16)
    messages = jnp.concatenate([messages[:EDGES], messages[EDGES:]], axis=1)
    node_rows[...] = jnp.dot(selector, messages, preferred_element_type=F32).astype(BF16)
    store_n = pltpu.make_async_copy(node_rows, node_out, out_sem.at[0])
    store_n.start()
    c = edge_cot[0]
    products = nt_dot(jnp.concatenate([c[:, :half], c[:, half:]], axis=0), matrix)
    grad_rows[:, :half] = (products[:EDGES, :half] + products[EDGES:, half:]).astype(BF16)
    grad_rows[:, half:] = (products[EDGES:, :half] - products[:EDGES, half:]).astype(BF16)
    store_e = pltpu.make_async_copy(grad_rows, edge_grad, out_sem.at[1])
    store_e.start()

    arrived(weight_out.at[pl.ds(0, 14)], ag_r)

    arrived(sum_recv.at[pl.ds(0, NZ - 1)], cz_r)
    summed = jnp.sum(sum_recv[...], axis=0)
    coef_out[...] = jnp.concatenate(
        [summed[a : a + 1, b * EXPERTS : (b + 1) * EXPERTS] for a in range(4) for b in range(4)], axis=0
    )

    sent(merged_send.at[pl.ds(0, NZ - 1)], fz_s)
    sent(merged_send, fy_s)
    sent(merged_send, fc_s)
    sent(merged_send, gc_s)
    sent(coef_all.at[pl.ds(0, NG - 1)], co_s)
    sent(z_send.at[pl.ds(0, NZ - 1)], bz_s)
    for group in range(2):
        sent(dp_send.at[group, pl.ds(0, NG - 1)], da_s.at[group])
    sent(weight_out.at[pl.ds(0, 14)], ag_s)
    sent(sum_recv.at[pl.ds(0, NZ - 1)], cz_s)
    feats_copy.wait_send()
    cot_copy.wait_send()
    core_part.wait_send()
    y_part.wait_send()
    for chunk in range(YC):
        ys(chunk).wait_send()
    store_n.wait()
    store_e.wait()
    store_w.wait()


def finish(
    node_rows, grad_rows, gathered, coef_rows, node_out, edge_grad, weight_out, coef_out,
    tiles, wide, node_held, grad_held, coef_held, sem, in_sem, out_sem,
):
    per = ROWS // PARTS
    moves = [
        (pltpu.make_async_copy(src, held, sem.at[n]), pltpu.make_async_copy(held, dst, sem.at[3 + n]))
        for n, (src, held, dst) in enumerate(
            ((node_rows, node_held, node_out), (grad_rows, grad_held, edge_grad), (coef_rows, coef_held, coef_out))
        )
    ]
    loads = [
        pltpu.make_async_copy(gathered.at[pl.ds(n * per, per)], tiles.at[pl.ds(n * per, per)], in_sem.at[n])
        for n in range(PARTS)
    ]
    for load in loads:
        load.start()
    for load, _ in moves:
        load.start()
    stores = []
    for n in range(PARTS):
        loads[n].wait()
        for row in range(n * per, n * per + per):
            for tile in range(NX):
                wide[:, pl.ds((row * NX + tile) * 128, 128)] = tiles[row, tile].astype(F32)
        lanes = pl.ds(n * per * COLS, per * COLS)
        stores.append(pltpu.make_async_copy(wide.at[:, lanes], weight_out.at[:, lanes], out_sem.at[n]))
        stores[n].start()
    for load, store in moves:
        load.wait()
        store.start()
    for store in [store for _, store in moves] + stores:
        store.wait()


def per_device(edge_feats, edge_dst, edge_live, coefficients, expert_weights, node_cot):
    vmem = pl.BlockSpec(memory_space=pltpu.VMEM)
    smem = pl.BlockSpec(memory_space=pltpu.SMEM)
    hbm = pl.BlockSpec(memory_space=pl.ANY)
    node_rows, grad_rows, gathered, coef_rows = pl.pallas_call(
        kernel,
        out_shape=(
            jax.ShapeDtypeStruct((EDGES, WIDTH), BF16),
            jax.ShapeDtypeStruct((EDGES, WIDTH), BF16),
            jax.ShapeDtypeStruct((ROWS, NX, EXPERTS, 128), BF16),
            jax.ShapeDtypeStruct((NZ, EXPERTS), F32),
        ),
        in_specs=[hbm, hbm, smem, hbm, hbm, hbm],
        out_specs=(hbm, hbm, hbm, vmem),
        scratch_shapes=[
            pltpu.VMEM((EXPERTS, ROWS * COLS), F32),
            pltpu.VMEM((EXPERTS, ROWS * COLS), BF16),
            pltpu.VMEM((NZ, EXPERTS), F32),
            pltpu.VMEM((1, EDGES), jnp.int32),
            pltpu.VMEM((NZ, ROWS, COLS), F32),
            pltpu.VMEM((NZ, ROWS, COLS), BF16),
            pltpu.VMEM((NZ, NQ, ROWS, COLS), BF16),
            pltpu.VMEM((2, EDGES, WIDTH), BF16),
            pltpu.VMEM((EDGES, WIDTH), BF16),
            pltpu.VMEM((2, EDGES, WIDTH), BF16),
            pltpu.VMEM((NZ, 2, 2, ROWS, COLS), F32),
            pltpu.VMEM((NZ, ROWS, COLS), BF16),
            pltpu.VMEM((NZ, ROWS, COLS), BF16),
            pltpu.VMEM((NZ, ROWS, COLS), BF16),
            pltpu.VMEM((NZ, ROWS, COLS), BF16),
            pltpu.VMEM((NZ, ROWS, COLS), F32),
            pltpu.VMEM((2, NG, 4, 16, 128), BF16),
            pltpu.VMEM((2, NG, 4, 16, 128), BF16),
            pltpu.VMEM((NZ * NG, 8, 128), F32),
            pltpu.VMEM((8, EXPERTS, 128), BF16),
            pltpu.VMEM((NG, NZ, 128), F32),
            pltpu.VMEM((NZ, 128), F32),
            pltpu.VMEM((4, 4, 128), F32),
            pltpu.VMEM((4, 128), F32),
            pltpu.VMEM((NZ, 4, 128), F32),
            pltpu.VMEM((EDGES, WIDTH), BF16),
            pltpu.VMEM((EDGES, WIDTH), BF16),
            DMA((5,)), DMA((3,)),
            DMA, DMA((len(GROUPS),)), DMA, DMA((len(GROUPS),)), DMA, DMA, DMA, DMA,
            DMA((2,)), DMA((2,)), DMA, DMA,
            DMA((YC,)), DMA((YC,)), DMA, DMA((2,)), DMA((2,)), DMA((2,)),
            DMA, DMA, DMA, DMA, DMA((2,)), DMA((2,)), pltpu.SemaphoreType.REGULAR,
        ],
        compiler_params=pltpu.CompilerParams(
            collective_id=0, has_side_effects=True, vmem_limit_bytes=60 * 1024 * 1024
        ),
    )(edge_feats, edge_dst.reshape(1, EDGES), edge_live, coefficients, expert_weights, node_cot)
    return pl.pallas_call(
        finish,
        out_shape=(
            jax.ShapeDtypeStruct((EDGES, WIDTH), BF16),
            jax.ShapeDtypeStruct((EDGES, WIDTH), BF16),
            jax.ShapeDtypeStruct((EXPERTS, ROWS * COLS), F32),
            jax.ShapeDtypeStruct((NZ, EXPERTS), F32),
        ),
        in_specs=[hbm, hbm, hbm, hbm],
        out_specs=(hbm, hbm, hbm, hbm),
        scratch_shapes=[
            pltpu.VMEM((ROWS, NX, EXPERTS, 128), BF16),
            pltpu.VMEM((EXPERTS, ROWS * COLS), F32),
            pltpu.VMEM((EDGES, WIDTH), BF16),
            pltpu.VMEM((EDGES, WIDTH), BF16),
            pltpu.VMEM((NZ, EXPERTS), F32),
            DMA((6,)), DMA((PARTS,)), DMA((PARTS,)),
        ],
        compiler_params=pltpu.CompilerParams(vmem_limit_bytes=FINISH_LIMIT * 1024 * 1024),
    )(node_rows, grad_rows, gathered, coef_rows)


def solution(mesh):
    in_specs = (
        P(("dp", "shard"), None),
        P(("dp", "shard")),
        P(("dp", "shard")),
        P("dp", None),
        P(None, "shard"),
        P(("dp", "shard"), None),
    )
    out_specs = (
        P(("dp", "shard"), None),
        P(("dp", "shard"), None),
        P(None, "shard"),
        P("dp", None),
    )
    return jax.shard_map(
        per_device, mesh=mesh, in_specs=in_specs, out_specs=out_specs, check_vma=False
    )
```

```python
import jax
import jax.numpy as jnp
from jax import lax
from jax.experimental import pallas as pl
from jax.experimental.pallas import tpu as pltpu
from jax.sharding import PartitionSpec as P

F32, BF16 = jnp.float32, jnp.bfloat16
NZ, NQ, NG = 16, 4, 8
NX = 4
ROWS, COLS = 16, 512
EDGES, WIDTH, EXPERTS = 128, 1024, 32
YC = 8
PER = NZ // YC
OFFS = [8, 7, 9, 6, 10, 5, 11, 4, 12, 3, 13, 2, 14, 1, 15, 0]
FIRST, SECOND, THIRD = [4, 12, 3, 13, 2, 14, 1, 15], [8, 7, 9], [5, 11, 6, 10]
GROUPS = [[0, 4, 12, 3, 13, 2, 14, 1, 15], [8, 7, 9], [5, 11], [6, 10]]
NEAR = [4, 12, 3, 13, 2, 14, 1, 15]
PARTS = 4
FINISH_LIMIT = 60
GROUP_OF = {off: group for group, offs in enumerate(GROUPS) for off in offs}
DMA = pltpu.SemaphoreType.DMA


def three_parts(value):
    high = value.astype(BF16)
    rest = value - high.astype(F32)
    middle = rest.astype(BF16)
    low = (rest - middle.astype(F32)).astype(BF16)
    return high, middle, low


def tn_dot(a, b):
    return lax.dot_general(a, b, (((0,), (0,)), ((), ())), preferred_element_type=F32)


def nt_dot(a, b):
    return lax.dot_general(a, b, (((1,), (1,)), ((), ())), preferred_element_type=F32)


def kernel(
    feats_in, dst_in, live_in, coef_in, weights_in, cot_in,
    node_out, edge_grad, weight_out, coef_out,
    weights, copies, coef, dst, merged_rows, merged_send, block, feats, node_cot, edge_cot,
    grads, y_send, y_recv, z_send, z_recv, z_wide, dp_send, dp_recv, crystals,
    gather_send, coef_all, planes, part, sum_send, sum_recv,
    node_rows, grad_rows,
    in_sem, out_sem, fz_s, fz_r, fy_s, fy_r, fc_s, fc_r, gc_s, gc_r, ex_s, ex_r, co_s, co_r,
    ys_s, ys_r, bz_s, bz_r, da_s, da_r, ag_s, ag_r, cz_s, cz_r, pt_s, pt_r, far_sem,
):
    g = lax.axis_index("dp")
    s = lax.axis_index("shard")
    z = s // NQ
    q = s % NQ
    yh = q // 2
    core = q % 2
    h = g // NX
    x = g % NX
    q_y = (1 - yh) * 2 + core
    q_c = yh * 2 + (1 - core)
    q_yc = (1 - yh) * 2 + (1 - core)
    core_peer = z * NQ + q_c
    y_peer = z * NQ + q_y
    half = WIDTH // 2

    load_w = pltpu.make_async_copy(weights_in, weights, in_sem.at[0])
    load_f = pltpu.make_async_copy(feats_in, feats.at[0], in_sem.at[1])
    load_c = pltpu.make_async_copy(cot_in, node_cot, in_sem.at[2])
    load_k = pltpu.make_async_copy(coef_in, coef, in_sem.at[3])
    load_d = pltpu.make_async_copy(dst_in, dst, in_sem.at[4])
    for load in (load_d, load_c, load_f, load_k, load_w):
        load.start()

    def copy_to(src, dst, send, recv, dp, shard):
        return pltpu.make_async_remote_copy(
            src_ref=src, dst_ref=dst, send_sem=send, recv_sem=recv,
            device_id={"dp": dp, "shard": shard}, device_id_type=pl.DeviceIdType.MESH,
        )

    def shard_copy(src, dst, send, recv, peer):
        return copy_to(src, dst, send, recv, g, peer)

    def dp_copy(src, dst, send, recv, peer):
        return copy_to(src, dst, send, recv, peer, s)

    def sent(ref, sem):
        shard_copy(ref, ref, sem, sem, core_peer).wait_send()

    def arrived(ref, sem):
        shard_copy(ref, ref, sem, sem, core_peer).wait_recv()

    def ahead(off):
        return (z + off) % NZ

    def behind(off):
        return (z + NZ - off) % NZ

    barrier = pltpu.get_barrier_semaphore()

    def greet(dp, shard):
        pl.semaphore_signal(
            barrier, inc=1, device_id={"dp": dp, "shard": shard}, device_id_type=pl.DeviceIdType.MESH
        )

    for off in NEAR:
        greet(g, ahead(off) * NQ + q)
    for off in range(1, NG):
        greet((g + off) % NG, s)
    greet(g, core_peer)
    greet(g, y_peer)

    load_d.wait()
    atom = lax.broadcasted_iota(jnp.int32, (EDGES, EDGES), 0)
    slot = lax.broadcasted_iota(jnp.int32, (EDGES, EDGES), 1)
    chosen = (dst[...] == atom) & (slot < live_in[0])
    selector = jnp.where(chosen, 1.0, 0.0).astype(BF16)
    load_c.wait()
    edge_cot[0] = tn_dot(selector, node_cot[...]).astype(BF16)
    load_f.wait()

    pl.semaphore_wait(barrier, 2 + len(NEAR) + (NG - 1))
    for off in (4, NZ - 4):
        pl.semaphore_signal(
            far_sem, inc=1, device_id={"dp": g, "shard": ahead(off) * NQ + q}, device_id_type=pl.DeviceIdType.MESH
        )

    feats_copy = shard_copy(feats.at[0], feats.at[1], ex_s.at[0], ex_r.at[0], core_peer)
    cot_copy = shard_copy(edge_cot.at[0], edge_cot.at[1], ex_s.at[1], ex_r.at[1], core_peer)
    feats_copy.start()
    cot_copy.start()

    load_k.wait()
    stacked = jnp.concatenate(three_parts(coef[...]), axis=0)
    blank = jnp.zeros((1, 128 - EXPERTS), F32)
    for j in range(NZ):
        row = coef[pl.ds(behind(OFFS[j]), 1), :]
        coef_all[g, pl.ds(j, 1), :] = jnp.concatenate([row, blank], axis=1)
    load_w.wait()
    for row in range(ROWS):
        lanes = pl.ds(row * COLS, COLS)
        rounded = weights[:, lanes].astype(BF16)
        copies[:, lanes] = rounded
        terms = jnp.dot(stacked, rounded, preferred_element_type=F32)
        merged_rows[:, row, :] = terms[0:NZ] + terms[NZ : 2 * NZ] + terms[2 * NZ : 3 * NZ]
    merged_send[...] = merged_rows[...].astype(BF16)
    block[z, q] = merged_send[z]

    def fz(off):
        to = ahead(off)
        return shard_copy(merged_send.at[to], block.at[z, q], fz_s, fz_r.at[GROUP_OF[off]], to * NQ + q)

    for off in FIRST:
        fz(off).start()
    for off in range(1, NG):
        dp_copy(coef_all.at[g], coef_all.at[g], co_s, co_r, (g + off) % NG).start()

    feats_copy.wait_recv()
    cot_copy.wait_recv()
    left, right = [], []
    for device in range(2):
        f, c = feats[device], edge_cot[device]
        left += [f[:, :half], f[:, half:]]
        right += [
            jnp.concatenate([c[:, :half], c[:, half:]], axis=1),
            jnp.concatenate([c[:, half:], -c[:, :half]], axis=1),
        ]
    outer = tn_dot(jnp.concatenate(left, axis=0), jnp.concatenate(right, axis=0)) * (1.0 / EDGES)
    grads[0 : NZ // 2] = outer[:, :half].reshape(NZ // 2, 2, 2, ROWS, COLS)
    grads[NZ // 2 : NZ] = outer[:, half:].reshape(NZ // 2, 2, 2, ROWS, COLS)

    def ys(chunk):
        at = pl.ds(chunk * PER, PER)
        return shard_copy(y_send.at[at], y_recv.at[at], ys_s.at[chunk], ys_r.at[chunk], y_peer)

    for chunk in range(YC):
        for j in range(chunk * PER, chunk * PER + PER):
            y_send[j] = grads[ahead(OFFS[j]), 1 - yh, core].astype(BF16)
        ys(chunk).start()

    pl.semaphore_wait(far_sem, 2)
    for off in SECOND:
        fz(off).start()

    for chunk in range(YC):
        ys(chunk).wait_recv()
        for j in range(chunk * PER, chunk * PER + PER):
            to = ahead(OFFS[j])
            z_send[j] = (grads[to, yh, core] + y_recv[j].astype(F32)).astype(BF16)
            if j < NZ - 1:
                shard_copy(z_send.at[j], z_recv.at[j], bz_s, bz_r.at[j // 8], to * NQ + q).start()
    z_recv[NZ - 1] = z_send[NZ - 1]

    for off in THIRD:
        fz(off).start()

    def forward(group):
        away = [off for off in GROUPS[group] if off > 0]
        arrived(merged_send.at[pl.ds(0, len(away))], fz_r.at[group])
        for off in GROUPS[group]:
            piece = block.at[behind(off), q]
            shard_copy(piece, piece, fy_s, fy_r.at[group], y_peer).start()
            shard_copy(piece, piece, fc_s, fc_r, core_peer).start()

    def forward_again(group):
        arrived(merged_send.at[pl.ds(0, len(GROUPS[group]))], fy_r.at[group])
        for off in GROUPS[group]:
            piece = block.at[behind(off), q_y]
            shard_copy(piece, piece, gc_s, gc_r, core_peer).start()

    def own_slice(group):
        slots = slice(group * 8, group * 8 + 8)
        wide = z_recv[slots].astype(F32)
        for to in range(NG):
            rows = slice((to // NX) * 8, (to // NX) * 8 + 8)
            lanes = slice((to % NX) * 128, (to % NX) * 128 + 128)
            for m in range(4):
                dp_send[group, to, m] = jnp.concatenate(
                    [wide[2 * m, rows, lanes], wide[2 * m + 1, rows, lanes]], axis=0
                ).astype(BF16)
        for off in range(1, NG):
            to = (g + off) % NG
            dp_copy(dp_send.at[group, to], dp_recv.at[group, g], da_s.at[group], da_r.at[group], to).start()
        dp_recv[group, g] = dp_send[group, g]
        z_wide[slots] = wide
        flat = jnp.concatenate([z_wide[slots, row, :] for row in range(ROWS)], axis=1).astype(BF16)
        found = nt_dot(flat, copies[...])
        for j in range(8):
            planes[pl.ds(behind(OFFS[group * 8 + j]), 1), :] = jnp.concatenate([found[j : j + 1], blank], axis=1)

    for group in range(2):
        forward(group)
    arrived(z_recv.at[pl.ds(0, 8)], bz_r.at[0])
    own_slice(0)
    arrived(z_recv.at[pl.ds(0, 7)], bz_r.at[1])
    own_slice(1)

    part[0] = jnp.concatenate([planes[pl.ds(b, 4, stride=4), :][:, :EXPERTS] for b in range(4)], axis=1)
    core_part = shard_copy(part.at[0], part.at[1], pt_s.at[0], pt_r.at[0], core_peer)
    core_part.start()
    core_part.wait_recv()
    part[2] = part[0] + part[1]
    y_part = shard_copy(part.at[2], part.at[3], pt_s.at[1], pt_r.at[1], y_peer)
    y_part.start()

    forward(2)

    forward(3)
    arrived(coef_all.at[pl.ds(0, NG - 1)], co_r)
    all_coef = jnp.concatenate(
        [coef_all[:, 0:8, :].reshape(64, 128), coef_all[:, 8:16, :].reshape(64, 128)], axis=0
    )[:, :EXPERTS]
    all_parts = jnp.concatenate(three_parts(all_coef), axis=1)
    for group in range(2):
        arrived(dp_recv.at[group, pl.ds(0, NG - 1)], da_r.at[group])
    crystals[...] = dp_recv[...].astype(F32).reshape(NZ * NG, 8, 128)
    flat = jnp.concatenate([crystals[:, row, :] for row in range(8)], axis=1).astype(BF16)
    terms = tn_dot(all_parts, flat)
    total = (terms[:EXPERTS] + terms[EXPERTS : 2 * EXPERTS] + terms[2 * EXPERTS :]).astype(BF16)
    for row in range(8):
        gather_send[row] = total[:, row * 128 : row * 128 + 128]
    own_rows = pl.ds(h * 8, 8)
    for off in (6, 2, 5, 7, 1, 3, 4):
        dp_copy(gather_send, weight_out.at[own_rows, x], ag_s, ag_r, (g + off) % NG).start()
    store_w = pltpu.make_async_copy(gather_send, weight_out.at[own_rows, x], out_sem.at[2])
    store_w.start()

    y_part.wait_recv()
    sum_send[...] = part[2] + part[3]
    for off in OFFS[:-1]:
        shard_copy(sum_send, sum_recv.at[z], cz_s, cz_r, ahead(off) * NQ + q).start()
    sum_recv[z] = sum_send[...]

    for group in range(len(GROUPS)):
        forward_again(group)
    arrived(merged_send, fc_r)
    arrived(merged_send, gc_r)

    matrix = block[...].reshape(NZ * NQ * ROWS, COLS)
    f = feats[0]
    lifted = jnp.concatenate(
        [
            jnp.concatenate([f[:, :half], -f[:, half:]], axis=1),
            jnp.concatenate([f[:, half:], f[:, :half]], axis=1),
        ],
        axis=0,
    )
    messages = jnp.dot(lifted, matrix, preferred_element_type=F32).astype(BF16)
    messages = jnp.concatenate([messages[:EDGES], messages[EDGES:]], axis=1)
    node_rows[...] = jnp.dot(selector, messages, preferred_element_type=F32).astype(BF16)
    store_n = pltpu.make_async_copy(node_rows, node_out, out_sem.at[0])
    store_n.start()
    c = edge_cot[0]
    products = nt_dot(jnp.concatenate([c[:, :half], c[:, half:]], axis=0), matrix)
    grad_rows[:, :half] = (products[:EDGES, :half] + products[EDGES:, half:]).astype(BF16)
    grad_rows[:, half:] = (products[EDGES:, :half] - products[:EDGES, half:]).astype(BF16)
    store_e = pltpu.make_async_copy(grad_rows, edge_grad, out_sem.at[1])
    store_e.start()

    arrived(weight_out.at[pl.ds(0, 14)], ag_r)

    arrived(sum_recv.at[pl.ds(0, NZ - 1)], cz_r)
    summed = jnp.sum(sum_recv[...], axis=0)
    coef_out[...] = jnp.concatenate(
        [summed[a : a + 1, b * EXPERTS : (b + 1) * EXPERTS] for a in range(4) for b in range(4)], axis=0
    )

    sent(merged_send.at[pl.ds(0, NZ - 1)], fz_s)
    sent(merged_send, fy_s)
    sent(merged_send, fc_s)
    sent(merged_send, gc_s)
    sent(coef_all.at[pl.ds(0, NG - 1)], co_s)
    sent(z_send.at[pl.ds(0, NZ - 1)], bz_s)
    for group in range(2):
        sent(dp_send.at[group, pl.ds(0, NG - 1)], da_s.at[group])
    sent(weight_out.at[pl.ds(0, 14)], ag_s)
    sent(sum_recv.at[pl.ds(0, NZ - 1)], cz_s)
    feats_copy.wait_send()
    cot_copy.wait_send()
    core_part.wait_send()
    y_part.wait_send()
    for chunk in range(YC):
        ys(chunk).wait_send()
    store_n.wait()
    store_e.wait()
    store_w.wait()


def finish(
    node_rows, grad_rows, gathered, coef_rows, node_out, edge_grad, weight_out, coef_out,
    tiles, wide, node_held, grad_held, coef_held, sem, in_sem, out_sem,
):
    per = ROWS // PARTS
    moves = [
        (pltpu.make_async_copy(src, held, sem.at[n]), pltpu.make_async_copy(held, dst, sem.at[3 + n]))
        for n, (src, held, dst) in enumerate(
            ((node_rows, node_held, node_out), (grad_rows, grad_held, edge_grad), (coef_rows, coef_held, coef_out))
        )
    ]
    loads = [
        pltpu.make_async_copy(gathered.at[pl.ds(n * per, per)], tiles.at[pl.ds(n * per, per)], in_sem.at[n])
        for n in range(PARTS)
    ]
    for load in loads:
        load.start()
    for load, _ in moves:
        load.start()
    stores = []
    for n in range(PARTS):
        loads[n].wait()
        for row in range(n * per, n * per + per):
            for tile in range(NX):
                wide[:, pl.ds((row * NX + tile) * 128, 128)] = tiles[row, tile].astype(F32)
        lanes = pl.ds(n * per * COLS, per * COLS)
        stores.append(pltpu.make_async_copy(wide.at[:, lanes], weight_out.at[:, lanes], out_sem.at[n]))
        stores[n].start()
    for load, store in moves:
        load.wait()
        store.start()
    for store in [store for _, store in moves] + stores:
        store.wait()


def per_device(edge_feats, edge_dst, edge_live, coefficients, expert_weights, node_cot):
    vmem = pl.BlockSpec(memory_space=pltpu.VMEM)
    smem = pl.BlockSpec(memory_space=pltpu.SMEM)
    hbm = pl.BlockSpec(memory_space=pl.ANY)
    node_rows, grad_rows, gathered, coef_rows = pl.pallas_call(
        kernel,
        out_shape=(
            jax.ShapeDtypeStruct((EDGES, WIDTH), BF16),
            jax.ShapeDtypeStruct((EDGES, WIDTH), BF16),
            jax.ShapeDtypeStruct((ROWS, NX, EXPERTS, 128), BF16),
            jax.ShapeDtypeStruct((NZ, EXPERTS), F32),
        ),
        in_specs=[hbm, hbm, smem, hbm, hbm, hbm],
        out_specs=(hbm, hbm, hbm, vmem),
        scratch_shapes=[
            pltpu.VMEM((EXPERTS, ROWS * COLS), F32),
            pltpu.VMEM((EXPERTS, ROWS * COLS), BF16),
            pltpu.VMEM((NZ, EXPERTS), F32),
            pltpu.VMEM((1, EDGES), jnp.int32),
            pltpu.VMEM((NZ, ROWS, COLS), F32),
            pltpu.VMEM((NZ, ROWS, COLS), BF16),
            pltpu.VMEM((NZ, NQ, ROWS, COLS), BF16),
            pltpu.VMEM((2, EDGES, WIDTH), BF16),
            pltpu.VMEM((EDGES, WIDTH), BF16),
            pltpu.VMEM((2, EDGES, WIDTH), BF16),
            pltpu.VMEM((NZ, 2, 2, ROWS, COLS), F32),
            pltpu.VMEM((NZ, ROWS, COLS), BF16),
            pltpu.VMEM((NZ, ROWS, COLS), BF16),
            pltpu.VMEM((NZ, ROWS, COLS), BF16),
            pltpu.VMEM((NZ, ROWS, COLS), BF16),
            pltpu.VMEM((NZ, ROWS, COLS), F32),
            pltpu.VMEM((2, NG, 4, 16, 128), BF16),
            pltpu.VMEM((2, NG, 4, 16, 128), BF16),
            pltpu.VMEM((NZ * NG, 8, 128), F32),
            pltpu.VMEM((8, EXPERTS, 128), BF16),
            pltpu.VMEM((NG, NZ, 128), F32),
            pltpu.VMEM((NZ, 128), F32),
            pltpu.VMEM((4, 4, 128), F32),
            pltpu.VMEM((4, 128), F32),
            pltpu.VMEM((NZ, 4, 128), F32),
            pltpu.VMEM((EDGES, WIDTH), BF16),
            pltpu.VMEM((EDGES, WIDTH), BF16),
            DMA((5,)), DMA((3,)),
            DMA, DMA((len(GROUPS),)), DMA, DMA((len(GROUPS),)), DMA, DMA, DMA, DMA,
            DMA((2,)), DMA((2,)), DMA, DMA,
            DMA((YC,)), DMA((YC,)), DMA, DMA((2,)), DMA((2,)), DMA((2,)),
            DMA, DMA, DMA, DMA, DMA((2,)), DMA((2,)), pltpu.SemaphoreType.REGULAR,
        ],
        compiler_params=pltpu.CompilerParams(
            collective_id=0, has_side_effects=True, vmem_limit_bytes=60 * 1024 * 1024
        ),
    )(edge_feats, edge_dst.reshape(1, EDGES), edge_live, coefficients, expert_weights, node_cot)
    return pl.pallas_call(
        finish,
        out_shape=(
            jax.ShapeDtypeStruct((EDGES, WIDTH), BF16),
            jax.ShapeDtypeStruct((EDGES, WIDTH), BF16),
            jax.ShapeDtypeStruct((EXPERTS, ROWS * COLS), F32),
            jax.ShapeDtypeStruct((NZ, EXPERTS), F32),
        ),
        in_specs=[hbm, hbm, hbm, hbm],
        out_specs=(hbm, hbm, hbm, hbm),
        scratch_shapes=[
            pltpu.VMEM((ROWS, NX, EXPERTS, 128), BF16),
            pltpu.VMEM((EXPERTS, ROWS * COLS), F32),
            pltpu.VMEM((EDGES, WIDTH), BF16),
            pltpu.VMEM((EDGES, WIDTH), BF16),
            pltpu.VMEM((NZ, EXPERTS), F32),
            DMA((6,)), DMA((PARTS,)), DMA((PARTS,)),
        ],
        compiler_params=pltpu.CompilerParams(vmem_limit_bytes=FINISH_LIMIT * 1024 * 1024),
    )(node_rows, grad_rows, gathered, coef_rows)


def solution(mesh):
    in_specs = (
        P(("dp", "shard"), None),
        P(("dp", "shard")),
        P(("dp", "shard")),
        P("dp", None),
        P(None, "shard"),
        P(("dp", "shard"), None),
    )
    out_specs = (
        P(("dp", "shard"), None),
        P(("dp", "shard"), None),
        P(None, "shard"),
        P("dp", None),
    )
    return jax.shard_map(
        per_device, mesh=mesh, in_specs=in_specs, out_specs=out_specs, check_vma=False
    )
```
